256 devices in a mesh: row: 64 (over z, y, core), col: 4 (over x).
Axes of the slice: x: 4, y: 4, z: 8, core: 2. Of those that a mesh axis runs over, the one named last changes fastest.
Arguments:
- panel_block: float32 [131072, 128], P(('row', 'col')), may hold values from -360 to 360
- trailing: float32 [131072, 2048], P('row', 'col'), may hold values from -2048 to 2048
Outputs:
- r_scaled: float32 [128, 128], replicated
- w_scaled: float32 [128, 2048], P(None, 'col')
- remainder: float32 [131072, 2048], P('row', 'col')
The draws below stay inside these ranges and needn't reach their ends.
All inputs are finite; a program needn't handle non-finite values.
Results may differ from the reference program's by a relative error of at most 0.0003.
Values sent between devices are 32-bit elements; how exact they have to be, the bound alone decides.
A program may use at most 64 MiB of HBM per device.

```python
import math
import jax
import jax.numpy as jnp
from jax import lax

NB = 128
CT = 2048
ROWS = 131072


def panel_values(key):
    key_list = jax.random.split(key, 3)
    values = jnp.clip(jax.random.normal(key_list[0], (ROWS, NB), jnp.float32), -4.0, 4.0)
    row_scale = jnp.exp(jax.random.uniform(key_list[1], (ROWS, 1), jnp.float32, 0.0, math.log(10.0)))
    rising = 1.0 + 2.0 * jnp.arange(ROWS, dtype=jnp.float32) / max(ROWS - 1, 1)
    row_scale = row_scale * rising[:, None]
    col_scale = jnp.exp(jax.random.uniform(key_list[2], (1, NB), jnp.float32, math.log(0.3), math.log(3.0)))
    return row_scale * col_scale * values


def draw_panel_block(key, part):
    return panel_values(jax.random.fold_in(key, 11))


def draw_trailing(key, part):
    base = panel_values(jax.random.fold_in(key, 11))
    mixing = jnp.clip(jax.random.normal(jax.random.fold_in(key, 23), (NB, CT), jnp.float32), -4.0, 4.0)
    mixing = mixing / (8.0 * math.sqrt(NB))
    noise_part = jnp.clip(jax.random.normal(jax.random.fold_in(key, 37), (ROWS, CT), jnp.float32), -4.0, 4.0)
    return jnp.dot(base, mixing, precision=lax.Precision.HIGHEST) + noise_part


def setup_inputs(seed: int = 0) -> dict:
    keys = jax.random.split(jax.random.key(seed), 3)
    panel_block = draw_panel_block(jax.random.fold_in(keys[2], 71), 0)
    trailing = draw_trailing(jax.random.fold_in(keys[2], 71), 0)
    return dict(panel_block=panel_block, trailing=trailing)


def reference(panel_block, trailing):
    basis, factor = jnp.linalg.qr(panel_block)
    sign_fix = jnp.sign(jnp.diagonal(factor))
    factor = factor * sign_fix[:, None]
    basis = basis * sign_fix[None, :]
    weights = jnp.dot(basis.T, trailing, precision=lax.Precision.HIGHEST)
    remainder = trailing - jnp.dot(basis, weights, precision=lax.Precision.HIGHEST)
    norm_scale = 1.0 / math.sqrt(ROWS)
    return (factor * norm_scale, weights * norm_scale, remainder)
```

```python
import math

import jax
import jax.numpy as jnp
from jax import lax
from jax.experimental import pallas as pl
from jax.experimental.pallas import tpu as pltpu
from jax.sharding import PartitionSpec as P

F32 = jnp.float32
BF16 = jnp.bfloat16
MESH = pl.DeviceIdType.MESH
HIGHEST = lax.Precision.HIGHEST
NB = 128
Y_DIM, Z_DIM, X_DIM = 4, 8, 4
CHIPS = Y_DIM * Z_DIM
ROWS_OWN = 512
COLS_OWN = 512
HALF = ROWS_OWN // 2


def reciprocal(p):
    r = pl.reciprocal(p, approx=True)
    return r * (2.0 - p * r)


def lane_spread(v, c):
    return jnp.broadcast_to(v[:, c : c + 1], (8, NB))


def row_spread(v, j):
    return jnp.broadcast_to(v[j : j + 1, :], (8, NB))


def factor_steps(g, r_ref, y_ref):
    sub = lax.broadcasted_iota(jnp.int32, (8, NB), 0)
    lane = lax.broadcasted_iota(jnp.int32, (8, NB), 1)
    n = NB // 8
    left = [g[i] for i in range(n)]
    right = [jnp.where(lane == sub + 8 * i, 1.0, 0.0) for i in range(n)]
    for k in range(n):
        v, w = left[k], right[k]
        diag = [lane_spread(v, 8 * k + j) for j in range(8)]
        more = k + 1 < n
        if more:
            diag2 = [lane_spread(left[k + 1], 8 * k + j) for j in range(8)]
            v2, w2 = left[k + 1], right[k + 1]
        pivots = jnp.ones((8, NB), F32)
        for j in range(8):
            p = row_spread(diag[j], j)
            r = reciprocal(p)
            m = jnp.where(sub > j, diag[j] * r, 0.0)
            vj, wj = row_spread(v, j), row_spread(w, j)
            v = v - m * vj
            w = w - m * wj
            if more:
                m2 = diag2[j] * r
                v2 = v2 - m2 * vj
                w2 = w2 - m2 * wj
            for jj in range(j + 1, 8):
                c = row_spread(diag[jj], j)
                diag[jj] = diag[jj] - m * c
                if more:
                    diag2[jj] = diag2[jj] - m2 * c
            pivots = jnp.where(sub == j, p, pivots)
        scale = lax.rsqrt(pivots)
        u = jnp.where(lane >= 8 * k + sub, v * scale, 0.0)
        z = w * scale
        r_ref[8 * k : 8 * k + 8, :] = u
        y_ref[8 * k : 8 * k + 8, :] = z
        if more:
            left[k + 1], right[k + 1] = v2, w2
        if k + 2 < n:
            ut = u.T
            us = [row_spread(u, j) for j in range(8)]
            zs = [row_spread(z, j) for j in range(8)]
            for i in range(k + 2, n):
                t = ut[8 * i : 8 * i + 8, :]
                a, b = left[i], right[i]
                for j in range(8):
                    tj = jnp.broadcast_to(t[:, j : j + 1], (8, NB))
                    a = a - tj * us[j]
                    b = b - tj * zs[j]
                left[i], right[i] = a, b
        yield


def split(x):
    hi = x.astype(BF16)
    return hi, (x - hi.astype(F32)).astype(BF16)


def inner(a, b, precision=None):
    return lax.dot_general(a, b, (((0,), (0,)), ((), ())), precision=precision, preferred_element_type=F32)


def main_kernel(
    p_hbm, t_hbm,
    r_ref, w_ref, xh_ref, xl_ref, phl_ref, t_ref,
    pg, thl, gbuf, abuf, bbuf, tile, gfull, y_ref, sbuf, cbuf, sred, rbuf, sfull,
    load_sem, gsend, grecv, esend, erecv,
):
    row = lax.axis_index("row")
    col = lax.axis_index("col")
    core = lax.rem(row, 2)
    chip = lax.div(row, 2)
    y = lax.rem(chip, Y_DIM)
    z = lax.div(chip, Y_DIM)
    right, left, across = (lax.rem(col + d, X_DIM) for d in (1, 3, 2))

    def device(z_, y_, core_):
        return (z_ * Y_DIM + y_) * 2 + core_

    sibling = (row + 1 - 2 * core, col)

    def zc_peer(d):
        q = lax.rem(z * 2 + core + d, 2 * Z_DIM)
        return q, (device(lax.div(q, 2), y, lax.rem(q, 2)), col)

    def yx_peer(d):
        s = lax.rem(y * X_DIM + col + d, Y_DIM * X_DIM)
        return s, (device(z, lax.div(s, X_DIM), core), lax.rem(s, X_DIM))

    def chip_peer(d):
        m = lax.rem(chip + d, CHIPS)
        return m, (m * 2 + core, col)

    me_q = z * 2 + core
    me_s = y * X_DIM + col

    def load_p():
        return pltpu.make_async_copy(p_hbm, pg.at[col], load_sem.at[4])

    def load_t(b, k):
        rows = pl.ds(pl.multiple_of(b * ROWS_OWN, ROWS_OWN), ROWS_OWN)
        return pltpu.make_async_copy(t_hbm.at[rows, :], t_ref.at[rows, :], load_sem.at[k])

    load_p().start()
    order = (col, left, right, across)
    for k, b in enumerate(order):
        load_t(b, k).start()

    barrier = pltpu.get_barrier_semaphore()

    def greet(peer):
        pl.semaphore_signal(barrier, inc=1, device_id=peer, device_id_type=MESH)

    def each(lo, hi, f):
        def step(d, c):
            f(d)
            return c

        lax.fori_loop(lo, hi, step, 0)

    each(1, CHIPS, lambda d: greet(chip_peer(d)[1]))
    each(0, Z_DIM, lambda d: greet((device(d, y, 1 - core), col)))
    each(1, X_DIM, lambda dx: each(0, Y_DIM, lambda d: greet((device(z, d, core), lax.rem(col + dx, X_DIM)))))

    load_p().wait()
    own = pg[col]
    gram = inner(own, own, HIGHEST)
    gbuf[...] = gram.reshape(NB // 8, 8, NB)
    pl.semaphore_wait(barrier, CHIPS - 1 + Z_DIM + (X_DIM - 1) * Y_DIM)

    def remote(src, dst, send, recv, peer):
        return pltpu.make_async_remote_copy(
            src_ref=src, dst_ref=dst, send_sem=send, recv_sem=recv, device_id=peer, device_id_type=MESH
        )

    def send_a(d):
        q, peer = zc_peer(d)
        remote(gbuf.at[q], abuf.at[d - 1], esend.at[0], erecv.at[0], peer).start()

    each(1, 2 * Z_DIM, send_a)

    top, bottom = pl.ds(0, HALF), pl.ds(HALF, HALF)

    def ring(k, block, part, to):
        return remote(pg.at[block, part, :], pg.at[block, part, :], gsend.at[k], grecv.at[k], (row, to))

    ring(0, col, top, right).start()
    ring(1, col, bottom, left).start()
    ring(2, col, bottom, right).start()
    ring(3, col, top, left).start()

    def split_t(k, b):
        load_t(b, k).wait()
        rows = pl.ds(pl.multiple_of(b * ROWS_OWN, ROWS_OWN), ROWS_OWN)
        hi, lo = split(t_ref[rows, :])
        thl[0, rows, :] = hi
        thl[1, rows, :] = lo

    def product(b, first=False):
        rows = pl.ds(pl.multiple_of(b * ROWS_OWN, ROWS_OWN), ROWS_OWN)
        hi, lo = split(pg[b])
        phl_ref[rows, 0:NB] = hi
        phl_ref[rows, NB : 2 * NB] = lo
        th = thl[0, rows, :]
        s = inner(hi, th) + inner(lo, th) + inner(hi, thl[1, rows, :])
        for j in range(4):
            t = s[:, NB * j : NB * (j + 1)].reshape(16, 8, NB)
            at = slice(16 * j, 16 * (j + 1))
            sbuf[at] = t if first else sbuf[at] + t

    split_t(0, order[0])
    product(col, True)

    def received(k, buf):
        remote(buf, buf, esend.at[k], erecv.at[k], sibling).wait_recv()

    def sent(k, buf):
        remote(buf, buf, esend.at[k], erecv.at[k], sibling).wait_send()

    n_zc, n_yx = 2 * Z_DIM - 1, Y_DIM * X_DIM - 1
    received(0, abuf)
    bbuf[me_s] = gbuf[me_q] + jnp.sum(abuf[...], axis=0)

    def send_b(d):
        _, peer = yx_peer(d)
        remote(bbuf.at[me_s], bbuf.at[me_s], esend.at[1], erecv.at[1], peer).start()

    each(1, n_yx + 1, send_b)

    split_t(1, order[1])
    split_t(2, order[2])

    ring(0, left, top, right).wait_recv()
    ring(4, left, top, right).start()
    ring(1, right, bottom, left).wait_recv()
    ring(5, right, bottom, left).start()

    received(1, bbuf.at[pl.ds(0, n_yx)])
    gfull[me_q] = jnp.sum(bbuf[...], axis=0)

    def send_c(d):
        _, peer = zc_peer(d)
        remote(gfull.at[me_q], gfull.at[me_q], esend.at[2], erecv.at[2], peer).start()

    each(1, n_zc + 1, send_c)

    split_t(3, order[3])
    ring(2, left, bottom, right).wait_recv()
    product(left)
    ring(3, right, top, left).wait_recv()
    product(right)

    received(2, gfull.at[pl.ds(0, n_zc)])
    steps = factor_steps([gfull[i] for i in range(NB // 8)], r_ref, y_ref)

    def factor(count):
        for _ in range(count):
            next(steps)

    factor(3)
    ring(4, across, top, right).wait_recv()
    ring(5, across, bottom, left).wait_recv()
    product(across)

    mine = pl.ds(pl.multiple_of(core * CHIPS, CHIPS), CHIPS)
    other = pl.ds(pl.multiple_of((1 - core) * CHIPS, CHIPS), CHIPS)
    swap = remote(sbuf.at[other], cbuf, esend.at[3], erecv.at[3], sibling)
    swap.start()
    factor(3)
    swap.wait_recv()
    sred[...] = sbuf[mine] + cbuf[...]

    def send_rs(d):
        m, peer = chip_peer(d)
        remote(sred.at[m], rbuf.at[d - 1], esend.at[4], erecv.at[4], peer).start()

    each(1, CHIPS, send_rs)
    factor(6)
    received(4, rbuf)
    slot = core * CHIPS + chip
    sfull[slot] = sred[chip] + jnp.sum(rbuf[...], axis=0)

    def send_ag(d):
        _, peer = chip_peer(d)
        remote(sfull.at[slot], sfull.at[slot], esend.at[5], erecv.at[5], peer).start()

    each(1, CHIPS, send_ag)
    factor(4)
    received(5, sfull.at[pl.ds(0, CHIPS - 1)])
    last = remote(sfull.at[mine], sfull.at[mine], esend.at[6], erecv.at[6], sibling)
    last.start()

    for k, block, part, to in (
        (0, col, top, right), (1, col, bottom, left), (2, col, bottom, right),
        (3, col, top, left), (4, left, top, right), (5, right, bottom, left),
    ):
        ring(k, block, part, to).wait_send()
    sent(0, abuf)
    sent(1, bbuf.at[pl.ds(0, n_yx)])
    sent(2, gfull.at[pl.ds(0, n_zc)])
    swap.wait_send()
    sent(4, rbuf)
    sent(5, sfull.at[pl.ds(0, CHIPS - 1)])

    last.wait()
    s = jnp.concatenate([sfull[16 * j : 16 * (j + 1)].reshape(NB, NB) for j in range(4)], axis=1)
    inv_t = y_ref[...]
    w = jnp.dot(inv_t, s, precision=HIGHEST, preferred_element_type=F32)
    w_ref[...] = w
    hi, lo = split(inner(inv_t, w, HIGHEST))
    xh_ref[...] = hi
    xl_ref[...] = lo


def rest_kernel(norm_scale, r_ref, w_ref, xh_ref, xl_ref, phl_ref, t_ref, rs_ref, ws_ref, out_hbm, obuf, sem, tiles=8):
    size = ROWS_OWN * X_DIM // tiles

    def put(i):
        return pltpu.make_async_copy(obuf.at[i], out_hbm.at[pl.ds(i * size, size), :], sem.at[i])

    for i in range(tiles):
        rows = slice(i * size, (i + 1) * size)
        ph, pl_ = phl_ref[rows, 0:NB], phl_ref[rows, NB : 2 * NB]
        xh = xh_ref[...]
        q = jnp.dot(ph, xh, preferred_element_type=F32) + jnp.dot(pl_, xh, preferred_element_type=F32)
        q = q + jnp.dot(ph, xl_ref[...], preferred_element_type=F32)
        obuf[i] = t_ref[rows, :] - q
        put(i).start()
    rs_ref[...] = r_ref[...] * norm_scale
    ws_ref[...] = w_ref[...] * norm_scale
    for i in range(tiles):
        put(i).wait()


def body(panel_block, trailing):
    total_rows = panel_block.shape[0] * lax.axis_size("row") * lax.axis_size("col")
    norm_scale = 1.0 / math.sqrt(total_rows)
    rows = trailing.shape[0]
    vm = pl.BlockSpec(memory_space=pltpu.VMEM)
    anym = pl.BlockSpec(memory_space=pl.ANY)

    def out(shape, dtype):
        return jax.ShapeDtypeStruct(shape, dtype)

    parts = pl.pallas_call(
        main_kernel,
        out_shape=[
            out((NB, NB), F32), out((NB, COLS_OWN), F32), out((NB, COLS_OWN), BF16), out((NB, COLS_OWN), BF16),
            out((rows, 2 * NB), BF16), out((rows, COLS_OWN), F32),
        ],
        in_specs=[pl.BlockSpec(memory_space=pltpu.HBM)] * 2,
        out_specs=[vm] * 6,
        scratch_shapes=[
            pltpu.VMEM((X_DIM, ROWS_OWN, NB), F32),
            pltpu.VMEM((2, rows, COLS_OWN), BF16),
            pltpu.VMEM((16, 8, NB), F32),
            pltpu.VMEM((15, 8, NB), F32),
            pltpu.VMEM((16, 8, NB), F32),
            pltpu.VMEM((8, NB), F32),
            pltpu.VMEM((16, 8, NB), F32),
            pltpu.VMEM((NB, NB), F32),
            pltpu.VMEM((64, 8, NB), F32),
            pltpu.VMEM((32, 8, NB), F32),
            pltpu.VMEM((32, 8, NB), F32),
            pltpu.VMEM((31, 8, NB), F32),
            pltpu.VMEM((64, 8, NB), F32),
            pltpu.SemaphoreType.DMA((5,)),
            pltpu.SemaphoreType.DMA((6,)),
            pltpu.SemaphoreType.DMA((6,)),
            pltpu.SemaphoreType.DMA((7,)),
            pltpu.SemaphoreType.DMA((7,)),
        ],
        compiler_params=pltpu.CompilerParams(collective_id=0, has_side_effects=True, vmem_limit_bytes=40 << 20),
    )(panel_block, trailing)
    return pl.pallas_call(
        lambda *refs: rest_kernel(norm_scale, *refs),
        out_shape=[out((NB, NB), F32), out((NB, COLS_OWN), F32), out((rows, COLS_OWN), F32)],
        in_specs=[vm] * 6,
        out_specs=[vm, vm, anym],
        scratch_shapes=[pltpu.VMEM((8, rows // 8, COLS_OWN), F32), pltpu.SemaphoreType.DMA((8,))],
        compiler_params=pltpu.CompilerParams(vmem_limit_bytes=40 << 20),
    )(*parts)


def solution(mesh):
    in_specs = (P(("row", "col"), None), P("row", "col"))
    out_specs = (P(), P(None, "col"), P("row", "col"))
    return jax.shard_map(body, mesh=mesh, in_specs=in_specs, out_specs=out_specs, check_vma=False)
```

```python
import math

import jax
import jax.numpy as jnp
from jax import lax
from jax.experimental import pallas as pl
from jax.experimental.pallas import tpu as pltpu
from jax.sharding import PartitionSpec as P

F32 = jnp.float32
BF16 = jnp.bfloat16
MESH = pl.DeviceIdType.MESH
HIGHEST = lax.Precision.HIGHEST
NB = 128
Y_DIM, Z_DIM, X_DIM = 4, 8, 4
CHIPS = Y_DIM * Z_DIM
ROWS_OWN = 512
COLS_OWN = 512
HALF = ROWS_OWN // 2


def reciprocal(p):
    r = pl.reciprocal(p, approx=True)
    return r * (2.0 - p * r)


def lane_spread(v, c):
    return jnp.broadcast_to(v[:, c : c + 1], (8, NB))


def row_spread(v, j):
    return jnp.broadcast_to(v[j : j + 1, :], (8, NB))


def factor_steps(g, r_ref, y_ref):
    sub = lax.broadcasted_iota(jnp.int32, (8, NB), 0)
    lane = lax.broadcasted_iota(jnp.int32, (8, NB), 1)
    n = NB // 8
    left = [g[i] for i in range(n)]
    right = [jnp.where(lane == sub + 8 * i, 1.0, 0.0) for i in range(n)]
    for k in range(n):
        v, w = left[k], right[k]
        diag = [lane_spread(v, 8 * k + j) for j in range(8)]
        more = k + 1 < n
        if more:
            diag2 = [lane_spread(left[k + 1], 8 * k + j) for j in range(8)]
            v2, w2 = left[k + 1], right[k + 1]
        pivots = jnp.ones((8, NB), F32)
        for j in range(8):
            p = row_spread(diag[j], j)
            r = reciprocal(p)
            m = jnp.where(sub > j, diag[j] * r, 0.0)
            vj, wj = row_spread(v, j), row_spread(w, j)
            v = v - m * vj
            w = w - m * wj
            if more:
                m2 = diag2[j] * r
                v2 = v2 - m2 * vj
                w2 = w2 - m2 * wj
            for jj in range(j + 1, 8):
                c = row_spread(diag[jj], j)
                diag[jj] = diag[jj] - m * c
                if more:
                    diag2[jj] = diag2[jj] - m2 * c
            pivots = jnp.where(sub == j, p, pivots)
        scale = lax.rsqrt(pivots)
        u = jnp.where(lane >= 8 * k + sub, v * scale, 0.0)
        z = w * scale
        r_ref[8 * k : 8 * k + 8, :] = u
        y_ref[8 * k : 8 * k + 8, :] = z
        if more:
            left[k + 1], right[k + 1] = v2, w2
        if k + 2 < n:
            ut = u.T
            us = [row_spread(u, j) for j in range(8)]
            zs = [row_spread(z, j) for j in range(8)]
            for i in range(k + 2, n):
                t = ut[8 * i : 8 * i + 8, :]
                a, b = left[i], right[i]
                for j in range(8):
                    tj = jnp.broadcast_to(t[:, j : j + 1], (8, NB))
                    a = a - tj * us[j]
                    b = b - tj * zs[j]
                left[i], right[i] = a, b
        yield


def split(x):
    hi = x.astype(BF16)
    return hi, (x - hi.astype(F32)).astype(BF16)


def inner(a, b, precision=None):
    return lax.dot_general(a, b, (((0,), (0,)), ((), ())), precision=precision, preferred_element_type=F32)


def main_kernel(
    p_hbm, t_hbm,
    r_ref, w_ref, xh_ref, xl_ref, phl_ref, t_ref,
    pg, thl, gbuf, abuf, bbuf, gfull, y_ref, sbuf, cbuf, sred, rbuf, sfull,
    load_sem, gsend, grecv, esend, erecv, know_sem,
):
    row = lax.axis_index("row")
    col = lax.axis_index("col")
    core = lax.rem(row, 2)
    chip = lax.div(row, 2)
    y = lax.rem(chip, Y_DIM)
    z = lax.div(chip, Y_DIM)
    right, left, across = (lax.rem(col + d, X_DIM) for d in (1, 3, 2))

    def device(z_, y_, core_):
        return (z_ * Y_DIM + y_) * 2 + core_

    sibling = (row + 1 - 2 * core, col)

    def hops(n, d):
        return min(d, n - d)

    def far_first(n, m):
        pairs = [(i, j) for i in range(n) for j in range(m) if i or j]
        return sorted(pairs, key=lambda p: -hops(n, p[0]) - hops(m, p[1]))

    def chip_peer(d):
        z_, y_ = lax.rem(z + d[0], Z_DIM), lax.rem(y + d[1], Y_DIM)
        return z_ * Y_DIM + y_, (device(z_, y_, core), col)

    def zc_peer(d):
        z_ = lax.rem(z + d[0], Z_DIM)
        return (device(z_, y, 1 - core if d[1] else core), col)

    def yx_peer(d):
        y_, x_ = lax.rem(y + d[0], Y_DIM), lax.rem(col + d[1], X_DIM)
        return y_ * X_DIM + x_, (device(z, y_, core), x_)

    n_zc, n_yx = 2 * Z_DIM - 1, Y_DIM * X_DIM - 1
    me_q = z * 2 + core
    me_s = y * X_DIM + col

    def load_p():
        return pltpu.make_async_copy(p_hbm, pg.at[col], load_sem.at[4])

    def load_t(b, k):
        rows = pl.ds(pl.multiple_of(b * ROWS_OWN, ROWS_OWN), ROWS_OWN)
        return pltpu.make_async_copy(t_hbm.at[rows, :], t_ref.at[rows, :], load_sem.at[k])

    load_p().start()
    order = (col, left, right, across)
    for k, b in enumerate(order):
        load_t(b, k).start()

    barrier = pltpu.get_barrier_semaphore()

    def greet(peer):
        pl.semaphore_signal(barrier, inc=1, device_id=peer, device_id_type=MESH)

    def each(lo, hi, f):
        def step(d, c):
            f(d)
            return c

        lax.fori_loop(lo, hi, step, 0)

    def greet_z(d):
        z_ = lax.rem(z + d, Z_DIM)
        greet((device(z_, y, core), col))
        greet((device(z_, y, 1 - core), col))

    each(1, 3, greet_z)
    each(Z_DIM - 2, Z_DIM, greet_z)
    greet(sibling)
    each(1, X_DIM, lambda d: greet((row, lax.rem(col + d, X_DIM))))
    each(1, Y_DIM, lambda d: greet((device(z, lax.rem(y + d, Y_DIM), core), col)))

    load_p().wait()
    pl.semaphore_wait(barrier, 9 + X_DIM - 1 + Y_DIM - 1)

    def introduce(peer, k=0):
        pl.semaphore_signal(know_sem.at[k], inc=1, device_id=peer, device_id_type=MESH)

    def remote(src, dst, send, recv, peer):
        return pltpu.make_async_remote_copy(
            src_ref=src, dst_ref=dst, send_sem=send, recv_sem=recv, device_id=peer, device_id_type=MESH
        )

    top, bottom = pl.ds(0, HALF), pl.ds(HALF, HALF)

    def ring(k, block, part, to):
        return remote(pg.at[block, part, :], pg.at[block, part, :], gsend.at[k], grecv.at[k], (row, to))

    ring(0, col, top, right).start()
    ring(1, col, bottom, left).start()
    ring(2, col, bottom, right).start()
    ring(3, col, top, left).start()

    introduce((device(lax.rem(z + 2, Z_DIM), y, core), col))
    introduce((device(lax.rem(z + Z_DIM - 2, Z_DIM), y, core), col))
    each(1, X_DIM, lambda d: introduce((row, lax.rem(col + d, X_DIM))))

    own = pg[col]
    gram = inner(own, own, HIGHEST)
    gbuf[...] = gram.reshape(NB // 8, 8, NB)

    pl.semaphore_wait(know_sem.at[0], 2 + X_DIM - 1)
    each(1, Y_DIM, lambda d: introduce((device(z, lax.rem(y + d, Y_DIM), core), col), 1))

    for k, d in enumerate(far_first(Y_DIM, X_DIM)):
        t, peer = yx_peer(d)
        remote(gbuf.at[t], abuf.at[k], esend.at[0], erecv.at[0], peer).start()

    def split_t(k, b):
        load_t(b, k).wait()
        rows = pl.ds(pl.multiple_of(b * ROWS_OWN, ROWS_OWN), ROWS_OWN)
        hi, lo = split(t_ref[rows, :])
        thl[0, rows, :] = hi
        thl[1, rows, :] = lo

    def product(b, first=False):
        rows = pl.ds(pl.multiple_of(b * ROWS_OWN, ROWS_OWN), ROWS_OWN)
        hi, lo = split(pg[b])
        phl_ref[rows, 0:NB] = hi
        phl_ref[rows, NB : 2 * NB] = lo
        th = thl[0, rows, :]
        s = inner(hi, th) + inner(lo, th) + inner(hi, thl[1, rows, :])
        for j in range(4):
            t = s[:, NB * j : NB * (j + 1)].reshape(16, 8, NB)
            at = slice(16 * j, 16 * (j + 1))
            sbuf[at] = t if first else sbuf[at] + t

    split_t(0, order[0])
    product(col, True)

    def received(k, buf):
        remote(buf, buf, esend.at[k], erecv.at[k], sibling).wait_recv()

    def sent(k, buf):
        remote(buf, buf, esend.at[k], erecv.at[k], sibling).wait_send()

    ring(0, left, top, right).wait_recv()
    ring(4, left, top, right).start()
    ring(1, right, bottom, left).wait_recv()
    ring(5, right, bottom, left).start()

    split_t(1, order[1])
    split_t(2, order[2])
    split_t(3, order[3])

    received(0, abuf)
    bbuf[me_q] = gbuf[me_s] + jnp.sum(abuf[...], axis=0)

    for d in far_first(Z_DIM, 2):
        remote(bbuf.at[me_q], bbuf.at[me_q], esend.at[1], erecv.at[1], zc_peer(d)).start()

    ring(2, left, bottom, right).wait_recv()
    product(left)
    ring(3, right, top, left).wait_recv()
    product(right)

    ring(4, across, top, right).wait_recv()
    ring(5, across, bottom, left).wait_recv()
    product(across)

    mine = pl.ds(pl.multiple_of(core * CHIPS, CHIPS), CHIPS)
    other = pl.ds(pl.multiple_of((1 - core) * CHIPS, CHIPS), CHIPS)
    swap = remote(sbuf.at[other], cbuf, esend.at[3], erecv.at[3], sibling)
    swap.start()

    swap.wait_recv()
    sred[...] = sbuf[mine] + cbuf[...]

    pl.semaphore_wait(know_sem.at[1], Y_DIM - 1)
    for k, d in enumerate(far_first(Z_DIM, Y_DIM)):
        m, peer = chip_peer(d)
        remote(sred.at[m], rbuf.at[k], esend.at[4], erecv.at[4], peer).start()

    received(1, bbuf.at[pl.ds(0, n_zc)])
    gfull[me_s] = jnp.sum(bbuf[...], axis=0)

    for d in far_first(Y_DIM, X_DIM):
        remote(gfull.at[me_s], gfull.at[me_s], esend.at[2], erecv.at[2], yx_peer(d)[1]).start()

    received(4, rbuf)
    slot = core * CHIPS + chip
    sfull[slot] = sred[chip] + jnp.sum(rbuf[...], axis=0)

    for d in far_first(Z_DIM, Y_DIM):
        remote(sfull.at[slot], sfull.at[slot], esend.at[5], erecv.at[5], chip_peer(d)[1]).start()
    received(2, gfull.at[pl.ds(0, n_yx)])
    steps = factor_steps([gfull[i] for i in range(NB // 8)], r_ref, y_ref)

    def factor(count):
        for _ in range(count):
            next(steps)

    factor(16)

    for k, block, part, to in (
        (0, col, top, right), (1, col, bottom, left), (2, col, bottom, right),
        (3, col, top, left), (4, left, top, right), (5, right, bottom, left),
    ):
        ring(k, block, part, to).wait_send()
    sent(0, abuf)
    sent(1, bbuf.at[pl.ds(0, n_zc)])
    sent(2, gfull.at[pl.ds(0, n_yx)])
    swap.wait_send()
    sent(4, rbuf)

    inv_t = y_ref[...]
    both = jnp.concatenate([inv_t, inner(inv_t, inv_t, HIGHEST)], axis=0)

    def finish(h):
        tiles = [sfull[pl.ds(pl.multiple_of(h * CHIPS + 16 * j, 16), 16)].reshape(NB, NB) for j in range(2)]
        wx = jnp.dot(both, jnp.concatenate(tiles, axis=1), precision=HIGHEST, preferred_element_type=F32)
        at = pl.ds(pl.multiple_of(h * (COLS_OWN // 2), COLS_OWN // 2), COLS_OWN // 2)
        w_ref[:, at] = wx[:NB]
        hi, lo = split(wx[NB:])
        xh_ref[0:NB, at] = hi
        xh_ref[NB : 2 * NB, at] = hi
        xl_ref[:, at] = lo

    received(5, sfull.at[pl.ds(0, CHIPS - 1)])
    last = remote(sfull.at[mine], sfull.at[mine], esend.at[6], erecv.at[6], sibling)
    last.start()
    finish(core)
    sent(5, sfull.at[pl.ds(0, CHIPS - 1)])
    last.wait()
    finish(1 - core)


def rest_kernel(norm_scale, r_ref, w_ref, xh_ref, xl_ref, phl_ref, t_ref, rs_hbm, ws_hbm, out_hbm, rs, ws, obuf, sem, tiles=8):
    size = ROWS_OWN * X_DIM // tiles

    def put(i):
        return pltpu.make_async_copy(obuf.at[i], out_hbm.at[pl.ds(i * size, size), :], sem.at[i])

    scaled = [pltpu.make_async_copy(rs, rs_hbm, sem.at[tiles]), pltpu.make_async_copy(ws, ws_hbm, sem.at[tiles + 1])]
    rs[...] = r_ref[...] * norm_scale
    ws[...] = w_ref[...] * norm_scale
    for copy in scaled:
        copy.start()
    for i in range(tiles):
        rows = slice(i * size, (i + 1) * size)
        q = jnp.dot(phl_ref[rows, :], xh_ref[...], preferred_element_type=F32)
        q = q + jnp.dot(phl_ref[rows, 0:NB], xl_ref[...], preferred_element_type=F32)
        obuf[i] = t_ref[rows, :] - q
        put(i).start()
    for copy in scaled:
        copy.wait()
    for i in range(tiles):
        put(i).wait()


def body(panel_block, trailing):
    total_rows = panel_block.shape[0] * lax.axis_size("row") * lax.axis_size("col")
    norm_scale = 1.0 / math.sqrt(total_rows)
    rows = trailing.shape[0]
    vm = pl.BlockSpec(memory_space=pltpu.VMEM)
    anym = pl.BlockSpec(memory_space=pl.ANY)

    def out(shape, dtype):
        return jax.ShapeDtypeStruct(shape, dtype)

    parts = pl.pallas_call(
        main_kernel,
        out_shape=[
            out((NB, NB), F32), out((NB, COLS_OWN), F32), out((2 * NB, COLS_OWN), BF16), out((NB, COLS_OWN), BF16),
            out((rows, 2 * NB), BF16), out((rows, COLS_OWN), F32),
        ],
        in_specs=[pl.BlockSpec(memory_space=pltpu.HBM)] * 2,
        out_specs=[vm] * 6,
        scratch_shapes=[
            pltpu.VMEM((X_DIM, ROWS_OWN, NB), F32),
            pltpu.VMEM((2, rows, COLS_OWN), BF16),
            pltpu.VMEM((16, 8, NB), F32),
            pltpu.VMEM((15, 8, NB), F32),
            pltpu.VMEM((16, 8, NB), F32),
            pltpu.VMEM((16, 8, NB), F32),
            pltpu.VMEM((NB, NB), F32),
            pltpu.VMEM((64, 8, NB), F32),
            pltpu.VMEM((32, 8, NB), F32),
            pltpu.VMEM((32, 8, NB), F32),
            pltpu.VMEM((31, 8, NB), F32),
            pltpu.VMEM((64, 8, NB), F32),
            pltpu.SemaphoreType.DMA((5,)),
            pltpu.SemaphoreType.DMA((6,)),
            pltpu.SemaphoreType.DMA((6,)),
            pltpu.SemaphoreType.DMA((7,)),
            pltpu.SemaphoreType.DMA((7,)),
            pltpu.SemaphoreType.REGULAR((2,)),
        ],
        compiler_params=pltpu.CompilerParams(collective_id=0, has_side_effects=True, vmem_limit_bytes=40 << 20),
    )(*(pltpu.with_memory_space_constraint(a, pltpu.HBM) for a in (panel_block, trailing)))
    return pl.pallas_call(
        lambda *refs: rest_kernel(norm_scale, *refs),
        out_shape=[out((NB, NB), F32), out((NB, COLS_OWN), F32), out((rows, COLS_OWN), F32)],
        in_specs=[vm] * 6,
        out_specs=[anym] * 3,
        scratch_shapes=[
            pltpu.VMEM((NB, NB), F32), pltpu.VMEM((NB, COLS_OWN), F32),
            pltpu.VMEM((8, rows // 8, COLS_OWN), F32), pltpu.SemaphoreType.DMA((10,)),
        ],
        compiler_params=pltpu.CompilerParams(vmem_limit_bytes=40 << 20),
    )(*parts)


def solution(mesh):
    in_specs = (P(("row", "col"), None), P("row", "col"))
    out_specs = (P(), P(None, "col"), P("row", "col"))
    return jax.shard_map(body, mesh=mesh, in_specs=in_specs, out_specs=out_specs, check_vma=False)
```

```python
import math

import jax
import jax.numpy as jnp
from jax import lax
from jax.experimental import pallas as pl
from jax.experimental.pallas import tpu as pltpu
from jax.sharding import PartitionSpec as P

F32 = jnp.float32
BF16 = jnp.bfloat16
MESH = pl.DeviceIdType.MESH
HIGHEST = lax.Precision.HIGHEST
NB = 128
Y_DIM, Z_DIM, X_DIM = 4, 8, 4
CHIPS = Y_DIM * Z_DIM
ROWS_OWN = 512
COLS_OWN = 512
HALF = ROWS_OWN // 2


def lane_spread(v, c):
    return jnp.broadcast_to(v[:, c : c + 1], (8, NB))


def row_spread(v, j):
    return jnp.broadcast_to(v[j : j + 1, :], (8, NB))


def factor_gram(g, r_ref, y_ref):
    sub = lax.broadcasted_iota(jnp.int32, (8, NB), 0)
    lane = lax.broadcasted_iota(jnp.int32, (8, NB), 1)
    n = NB // 8
    left = [g[i] for i in range(n)]
    right = [jnp.where(lane == sub + 8 * i, 1.0, 0.0) for i in range(n)]
    for k in range(n):
        v, w = left[k], right[k]
        diag = [lane_spread(v, 8 * k + j) for j in range(8)]
        more = k + 1 < n
        if more:
            v2, w2 = left[k + 1], right[k + 1]
            diag2 = [lane_spread(v2, 8 * k + j) for j in range(8)]
        pivots = jnp.ones((8, NB), F32)
        p = row_spread(diag[0], 0)
        for j in range(8):
            r0 = pltpu.reciprocal(p, approx=True)
            e = 2.0 - p * r0
            r = r0 * e
            pivots = jnp.where(sub == j, p, pivots)
            rows = [row_spread(diag[jj], j) for jj in range(j + 1, 8)]
            if rows:
                p = row_spread(diag[j + 1], j + 1) - (rows[0] * rows[0] * r0) * e
            m = jnp.where(sub > j, diag[j], 0.0) * r
            vj, wj = row_spread(v, j), row_spread(w, j)
            v, w = v - m * vj, w - m * wj
            if more:
                m2 = diag2[j] * r
                v2, w2 = v2 - m2 * vj, w2 - m2 * wj
            for jj, row in zip(range(j + 1, 8), rows):
                diag[jj] = diag[jj] - m * row
                if more:
                    diag2[jj] = diag2[jj] - m2 * row
        scale = lax.rsqrt(pivots)
        u = jnp.where(lane >= 8 * k + sub, v * scale, 0.0)
        z = w * scale
        r_ref[8 * k : 8 * k + 8, :] = u
        y_ref[8 * k : 8 * k + 8, :] = z
        if more:
            left[k + 1], right[k + 1] = v2, w2
        if k + 2 < n:
            uz = jnp.concatenate([u, z], axis=1)
            high = uz.astype(BF16).astype(F32)
            mid = (uz - high).astype(BF16).astype(F32)
            low = uz - high - mid
            one = [high, high, mid, high, mid, low]
            two = [high, mid, high, low, mid, high]
            drop = inner(
                jnp.concatenate([q[:, :NB] for q in one], axis=0).astype(BF16),
                jnp.concatenate(two, axis=0).astype(BF16),
            )
            for i in range(k + 2, n):
                left[i] = left[i] - drop[8 * i : 8 * i + 8, :NB]
                right[i] = right[i] - drop[8 * i : 8 * i + 8, NB:]


def split(x):
    hi = x.astype(BF16)
    return hi, (x - hi.astype(F32)).astype(BF16)


def inner(a, b, precision=None):
    return lax.dot_general(a, b, (((0,), (0,)), ((), ())), precision=precision, preferred_element_type=F32)


def main_kernel(
    p_hbm, t_hbm,
    r_ref, w_ref, xh_ref, xl_ref, phl_ref, t_ref,
    pg, thl, gbuf, abuf, bbuf, gfull, y_ref, sbuf, cbuf, sred, rbuf, sfull,
    load_sem, gsend, grecv, esend, erecv, know_sem,
):
    row = lax.axis_index("row")
    col = lax.axis_index("col")
    core = lax.rem(row, 2)
    chip = lax.div(row, 2)
    y = lax.rem(chip, Y_DIM)
    z = lax.div(chip, Y_DIM)
    right, left, across = (lax.rem(col + d, X_DIM) for d in (1, 3, 2))

    def device(z_, y_, core_):
        return (z_ * Y_DIM + y_) * 2 + core_

    sibling = (row + 1 - 2 * core, col)

    def hops(n, d):
        return min(d, n - d)

    def far_first(n, m):
        pairs = [(i, j) for i in range(n) for j in range(m) if i or j]
        return sorted(pairs, key=lambda p: -hops(n, p[0]) - hops(m, p[1]))

    def chip_peer(d):
        z_, y_ = lax.rem(z + d[0], Z_DIM), lax.rem(y + d[1], Y_DIM)
        return z_ * Y_DIM + y_, (device(z_, y_, core), col)

    def zc_peer(d):
        z_ = lax.rem(z + d[0], Z_DIM)
        return (device(z_, y, 1 - core if d[1] else core), col)

    def yx_peer(d):
        y_, x_ = lax.rem(y + d[0], Y_DIM), lax.rem(col + d[1], X_DIM)
        return y_ * X_DIM + x_, (device(z, y_, core), x_)

    n_zc, n_yx = 2 * Z_DIM - 1, Y_DIM * X_DIM - 1
    me_q = z * 2 + core
    me_s = y * X_DIM + col

    def load_p():
        return pltpu.make_async_copy(p_hbm, pg.at[col], load_sem.at[4])

    def load_t(b, k):
        rows = pl.ds(pl.multiple_of(b * ROWS_OWN, ROWS_OWN), ROWS_OWN)
        return pltpu.make_async_copy(t_hbm.at[rows, :], t_ref.at[rows, :], load_sem.at[k])

    load_p().start()
    order = (col, left, right, across)
    for k, b in enumerate(order):
        load_t(b, k).start()

    barrier = pltpu.get_barrier_semaphore()

    def greet(peer):
        pl.semaphore_signal(barrier, inc=1, device_id=peer, device_id_type=MESH)

    def each(lo, hi, f):
        def step(d, c):
            f(d)
            return c

        lax.fori_loop(lo, hi, step, 0)

    z_next, z_prev = (lax.rem(z + d, Z_DIM) for d in (1, Z_DIM - 1))
    y_next, y_prev = (lax.rem(y + d, Y_DIM) for d in (1, Y_DIM - 1))
    near = (
        (row, right), (row, left), (device(z, y_next, core), col), (device(z, y_prev, core), col),
        (device(z_next, y, core), col), (device(z_prev, y, core), col),
    )
    for peer in near:
        greet(peer)
    greet(sibling)

    load_p().wait()
    pl.semaphore_wait(barrier, 7)

    def introduce(peer, k=0):
        pl.semaphore_signal(know_sem.at[k], inc=1, device_id=peer, device_id_type=MESH)

    def remote(src, dst, send, recv, peer):
        return pltpu.make_async_remote_copy(
            src_ref=src, dst_ref=dst, send_sem=send, recv_sem=recv, device_id=peer, device_id_type=MESH
        )

    top, bottom = pl.ds(0, HALF), pl.ds(HALF, HALF)

    def ring(k, block, part, to):
        src = pg.at[block, part, :]
        return remote(src, pg.at[block, part, :], gsend.at[k], grecv.at[k], (row, to))

    ring(0, col, top, right).start()
    ring(1, col, bottom, left).start()
    ring(2, col, bottom, right).start()
    ring(3, col, top, left).start()

    for peer in near:
        introduce(peer)

    own = pg[col]
    gram = inner(own, own, HIGHEST)
    gbuf[...] = gram.reshape(NB // 8, 8, NB)

    pl.semaphore_wait(know_sem.at[0], len(near))
    introduce((device(lax.rem(z + 2, Z_DIM), y, core), col), 1)
    introduce((device(lax.rem(z + Z_DIM - 2, Z_DIM), y, core), col), 1)
    for to in (right, left, across):
        introduce((row, to), 1)

    def split_t(k, b):
        load_t(b, k).wait()
        rows = pl.ds(pl.multiple_of(b * ROWS_OWN, ROWS_OWN), ROWS_OWN)
        hi, lo = split(t_ref[rows, :])
        thl[0, rows, :] = hi
        thl[1, rows, :] = lo

    def rows_of(b):
        return pl.ds(pl.multiple_of(b * ROWS_OWN, ROWS_OWN), ROWS_OWN)

    def split_p(b):
        hi, lo = split(pg[b])
        phl_ref[rows_of(b), 0:NB] = hi
        phl_ref[rows_of(b), NB : 2 * NB] = lo

    def product(b, h, first=False):
        at = pl.ds(pl.multiple_of(h * (COLS_OWN // 2), COLS_OWN // 2), COLS_OWN // 2)
        hi, lo = phl_ref[rows_of(b), 0:NB], phl_ref[rows_of(b), NB : 2 * NB]
        th = thl[0, rows_of(b), at]
        s = inner(hi, th) + inner(lo, th) + inner(hi, thl[1, rows_of(b), at])
        for j in range(2):
            t = s[:, NB * j : NB * (j + 1)].reshape(16, 8, NB)
            tiles = pl.ds(pl.multiple_of(h * CHIPS + 16 * j, 16), 16)
            sbuf[tiles] = t if first else sbuf[tiles] + t

    split_t(0, order[0])
    split_p(col)
    product(col, 0, True)
    product(col, 1, True)
    pl.semaphore_wait(know_sem.at[1], 2 + X_DIM - 1)
    each(1, Y_DIM, lambda d: introduce((device(z, lax.rem(y + d, Y_DIM), core), col), 2))
    introduce(sibling, 2)

    for k, d in enumerate(far_first(Y_DIM, X_DIM)):
        t, peer = yx_peer(d)
        remote(gbuf.at[t], abuf.at[k], esend.at[0], erecv.at[0], peer).start()

    def received(k, buf):
        remote(buf, buf, esend.at[k], erecv.at[k], sibling).wait_recv()

    def sent(k, buf):
        remote(buf, buf, esend.at[k], erecv.at[k], sibling).wait_send()

    ring(0, left, top, right).wait_recv()
    ring(4, left, top, right).start()
    ring(1, right, bottom, left).wait_recv()
    ring(5, right, bottom, left).start()

    split_t(1, order[1])
    split_t(2, order[2])
    split_t(3, order[3])

    received(0, abuf)
    bbuf[me_q] = gbuf[me_s] + jnp.sum(abuf[...], axis=0)

    pl.semaphore_wait(know_sem.at[2], Y_DIM)

    for d in far_first(Z_DIM, 2):
        remote(bbuf.at[me_q], bbuf.at[me_q], esend.at[1], erecv.at[1], zc_peer(d)).start()

    ring(2, left, bottom, right).wait_recv()
    split_p(left)
    product(left, 0)
    product(left, 1)
    ring(3, right, top, left).wait_recv()
    split_p(right)
    product(right, 0)
    product(right, 1)

    ring(4, across, top, right).wait_recv()
    ring(5, across, bottom, left).wait_recv()
    split_p(across)
    product(across, 1 - core)

    mine = pl.ds(pl.multiple_of(core * CHIPS, CHIPS), CHIPS)
    other = pl.ds(pl.multiple_of((1 - core) * CHIPS, CHIPS), CHIPS)
    swap = remote(sbuf.at[other], cbuf, esend.at[3], erecv.at[3], sibling)
    swap.start()
    product(across, core)
    swap.wait_recv()
    sred[...] = sbuf[mine] + cbuf[...]

    for k, d in enumerate(far_first(Z_DIM, Y_DIM)):
        m, peer = chip_peer(d)
        remote(sred.at[m], rbuf.at[k], esend.at[4], erecv.at[4], peer).start()

    received(1, bbuf.at[pl.ds(0, n_zc)])
    gfull[me_s] = jnp.sum(bbuf[...], axis=0)

    for d in far_first(Y_DIM, X_DIM):
        remote(gfull.at[me_s], gfull.at[me_s], esend.at[2], erecv.at[2], yx_peer(d)[1]).start()

    received(4, rbuf)
    slot = core * CHIPS + chip
    sfull[slot] = sred[chip] + jnp.sum(rbuf[...], axis=0)

    for d in far_first(Z_DIM, Y_DIM):
        remote(sfull.at[slot], sfull.at[slot], esend.at[5], erecv.at[5], chip_peer(d)[1]).start()
    received(2, gfull.at[pl.ds(0, n_yx)])
    factor_gram([gfull[i] for i in range(NB // 8)], r_ref, y_ref)

    for k, block, part, to in (
        (0, col, top, right), (1, col, bottom, left), (2, col, bottom, right),
        (3, col, top, left), (4, left, top, right), (5, right, bottom, left),
    ):
        ring(k, block, part, to).wait_send()
    sent(0, abuf)
    sent(1, bbuf.at[pl.ds(0, n_zc)])
    sent(2, gfull.at[pl.ds(0, n_yx)])
    swap.wait_send()
    sent(4, rbuf)

    inv_t = y_ref[...]
    both = jnp.concatenate([inv_t, inner(inv_t, inv_t, HIGHEST)], axis=0)

    def finish(h):
        tiles = [sfull[pl.ds(pl.multiple_of(h * CHIPS + 16 * j, 16), 16)].reshape(NB, NB) for j in range(2)]
        wx = jnp.dot(both, jnp.concatenate(tiles, axis=1), precision=HIGHEST, preferred_element_type=F32)
        at = pl.ds(pl.multiple_of(h * (COLS_OWN // 2), COLS_OWN // 2), COLS_OWN // 2)
        w_ref[:, at] = wx[:NB]
        hi, lo = split(wx[NB:])
        xh_ref[0:NB, at] = hi
        xh_ref[NB : 2 * NB, at] = hi
        xl_ref[:, at] = lo

    received(5, sfull.at[pl.ds(0, CHIPS - 1)])
    last = remote(sfull.at[mine], sfull.at[mine], esend.at[6], erecv.at[6], sibling)
    last.start()
    finish(core)
    sent(5, sfull.at[pl.ds(0, CHIPS - 1)])
    last.wait()
    finish(1 - core)


def rest_kernel(norm_scale, r_ref, w_ref, xh_ref, xl_ref, phl_ref, t_ref, rs_hbm, ws_hbm, out_hbm, rs, ws, obuf, sem, tiles=8):
    size = ROWS_OWN * X_DIM // tiles

    def put(i):
        return pltpu.make_async_copy(obuf.at[i], out_hbm.at[pl.ds(i * size, size), :], sem.at[i])

    scaled = [pltpu.make_async_copy(rs, rs_hbm, sem.at[tiles]), pltpu.make_async_copy(ws, ws_hbm, sem.at[tiles + 1])]
    rs[...] = r_ref[...] * norm_scale
    ws[...] = w_ref[...] * norm_scale
    for copy in scaled:
        copy.start()
    for i in range(tiles):
        rows = slice(i * size, (i + 1) * size)
        q = jnp.dot(phl_ref[rows, :], xh_ref[...], preferred_element_type=F32)
        q = q + jnp.dot(phl_ref[rows, 0:NB], xl_ref[...], preferred_element_type=F32)
        obuf[i] = t_ref[rows, :] - q
        put(i).start()
    for copy in scaled:
        copy.wait()
    for i in range(tiles):
        put(i).wait()


def body(panel_block, trailing):
    total_rows = panel_block.shape[0] * lax.axis_size("row") * lax.axis_size("col")
    norm_scale = 1.0 / math.sqrt(total_rows)
    rows = trailing.shape[0]
    vm = pl.BlockSpec(memory_space=pltpu.VMEM)
    anym = pl.BlockSpec(memory_space=pl.ANY)

    def out(shape, dtype):
        return jax.ShapeDtypeStruct(shape, dtype)

    parts = pl.pallas_call(
        main_kernel,
        out_shape=[
            out((NB, NB), F32), out((NB, COLS_OWN), F32), out((2 * NB, COLS_OWN), BF16), out((NB, COLS_OWN), BF16),
            out((rows, 2 * NB), BF16), out((rows, COLS_OWN), F32),
        ],
        in_specs=[pl.BlockSpec(memory_space=pltpu.HBM)] * 2,
        out_specs=[vm] * 6,
        scratch_shapes=[
            pltpu.VMEM((X_DIM, ROWS_OWN, NB), F32),
            pltpu.VMEM((2, rows, COLS_OWN), BF16),
            pltpu.VMEM((16, 8, NB), F32),
            pltpu.VMEM((15, 8, NB), F32),
            pltpu.VMEM((16, 8, NB), F32),
            pltpu.VMEM((16, 8, NB), F32),
            pltpu.VMEM((NB, NB), F32),
            pltpu.VMEM((64, 8, NB), F32),
            pltpu.VMEM((32, 8, NB), F32),
            pltpu.VMEM((32, 8, NB), F32),
            pltpu.VMEM((31, 8, NB), F32),
            pltpu.VMEM((64, 8, NB), F32),
            pltpu.SemaphoreType.DMA((5,)),
            pltpu.SemaphoreType.DMA((6,)),
            pltpu.SemaphoreType.DMA((6,)),
            pltpu.SemaphoreType.DMA((7,)),
            pltpu.SemaphoreType.DMA((7,)),
            pltpu.SemaphoreType.REGULAR((3,)),
        ],
        compiler_params=pltpu.CompilerParams(collective_id=0, has_side_effects=True, vmem_limit_bytes=40 << 20),
    )(*(pltpu.with_memory_space_constraint(a, pltpu.HBM) for a in (panel_block, trailing)))
    return pl.pallas_call(
        lambda *refs: rest_kernel(norm_scale, *refs),
        out_shape=[out((NB, NB), F32), out((NB, COLS_OWN), F32), out((rows, COLS_OWN), F32)],
        in_specs=[vm] * 6,
        out_specs=[anym] * 3,
        scratch_shapes=[
            pltpu.VMEM((NB, NB), F32), pltpu.VMEM((NB, COLS_OWN), F32),
            pltpu.VMEM((8, rows // 8, COLS_OWN), F32), pltpu.SemaphoreType.DMA((10,)),
        ],
        compiler_params=pltpu.CompilerParams(vmem_limit_bytes=40 << 20),
    )(*parts)


def solution(mesh):
    in_specs = (P(("row", "col"), None), P("row", "col"))
    out_specs = (P(), P(None, "col"), P("row", "col"))
    return jax.shard_map(body, mesh=mesh, in_specs=in_specs, out_specs=out_specs, check_vma=False)
```

```python
import math

import jax
import jax.numpy as jnp
from jax import lax
from jax.experimental import pallas as pl
from jax.experimental.pallas import tpu as pltpu
from jax.sharding import PartitionSpec as P

F32 = jnp.float32
BF16 = jnp.bfloat16
MESH = pl.DeviceIdType.MESH
HIGHEST = lax.Precision.HIGHEST
NB = 128
Y_DIM, Z_DIM, X_DIM = 4, 8, 4
CHIPS = Y_DIM * Z_DIM
ROWS_OWN = 512
COLS_OWN = 512
HALF = ROWS_OWN // 2


def lane_spread(v, c):
    return jnp.broadcast_to(v[:, c : c + 1], (8, NB))


def row_spread(v, j):
    return jnp.broadcast_to(v[j : j + 1, :], (8, NB))


def factor_gram(g, r_ref, y_ref):
    sub = lax.broadcasted_iota(jnp.int32, (8, NB), 0)
    lane = lax.broadcasted_iota(jnp.int32, (8, NB), 1)
    n = NB // 8
    left = [g[i] for i in range(n)]
    right = [jnp.where(lane == sub + 8 * i, 1.0, 0.0) for i in range(n)]
    for k in range(n):
        v, w = left[k], right[k]
        diag = [lane_spread(v, 8 * k + j) for j in range(8)]
        more = k + 1 < n
        if more:
            v2, w2 = left[k + 1], right[k + 1]
            diag2 = [lane_spread(v2, 8 * k + j) for j in range(8)]
        pivots = jnp.ones((8, NB), F32)
        p = row_spread(diag[0], 0)
        for j in range(8):
            r0 = pltpu.reciprocal(p, approx=True)
            e = 2.0 - p * r0
            r = r0 * e
            pivots = jnp.where(sub == j, p, pivots)
            rows = [row_spread(diag[jj], j) for jj in range(j + 1, 8)]
            if rows:
                p = row_spread(diag[j + 1], j + 1) - (rows[0] * rows[0] * r0) * e
            m = jnp.where(sub > j, diag[j], 0.0) * r
            vj, wj = row_spread(v, j), row_spread(w, j)
            v, w = v - m * vj, w - m * wj
            if more:
                m2 = diag2[j] * r
                v2, w2 = v2 - m2 * vj, w2 - m2 * wj
            for jj, row in zip(range(j + 1, 8), rows):
                diag[jj] = diag[jj] - m * row
                if more:
                    diag2[jj] = diag2[jj] - m2 * row
        scale = lax.rsqrt(pivots)
        u = jnp.where(lane >= 8 * k + sub, v * scale, 0.0)
        z = w * scale
        r_ref[8 * k : 8 * k + 8, :] = u
        y_ref[8 * k : 8 * k + 8, :] = z
        if more:
            left[k + 1], right[k + 1] = v2, w2
        if k + 2 < n:
            uz = jnp.concatenate([u, z], axis=1)
            high = uz.astype(BF16).astype(F32)
            mid = (uz - high).astype(BF16).astype(F32)
            low = uz - high - mid
            one = [high, high, mid, high, mid, low]
            two = [high, mid, high, low, mid, high]
            drop = inner(
                jnp.concatenate([q[:, :NB] for q in one], axis=0).astype(BF16),
                jnp.concatenate(two, axis=0).astype(BF16),
            )
            for i in range(k + 2, n):
                left[i] = left[i] - drop[8 * i : 8 * i + 8, :NB]
                right[i] = right[i] - drop[8 * i : 8 * i + 8, NB:]


def split(x):
    hi = x.astype(BF16)
    return hi, (x - hi.astype(F32)).astype(BF16)


def inner(a, b, precision=None):
    return lax.dot_general(a, b, (((0,), (0,)), ((), ())), precision=precision, preferred_element_type=F32)


def main_kernel(
    p_hbm, t_hbm,
    r_ref, w_ref, xh_ref, xl_ref, phl_ref, t_ref,
    pg, thl, gbuf, abuf, bbuf, gfull, y_ref, sbuf, cbuf, sred, rbuf, sfull,
    load_sem, gsend, grecv, esend, erecv, know_sem,
):
    row = lax.axis_index("row")
    col = lax.axis_index("col")
    core = lax.rem(row, 2)
    chip = lax.div(row, 2)
    y = lax.rem(chip, Y_DIM)
    z = lax.div(chip, Y_DIM)
    right, left, across = (lax.rem(col + d, X_DIM) for d in (1, 3, 2))

    def device(z_, y_, core_):
        return (z_ * Y_DIM + y_) * 2 + core_

    sibling = (row + 1 - 2 * core, col)

    def hops(n, d):
        return min(d, n - d)

    def far_first(n, m):
        pairs = [(i, j) for i in range(n) for j in range(m) if i or j]
        return sorted(pairs, key=lambda p: -hops(n, p[0]) - hops(m, p[1]))

    def chip_peer(d):
        z_, y_ = lax.rem(z + d[0], Z_DIM), lax.rem(y + d[1], Y_DIM)
        return z_ * Y_DIM + y_, (device(z_, y_, core), col)

    def zc_peer(d):
        z_ = lax.rem(z + d[0], Z_DIM)
        return (device(z_, y, 1 - core if d[1] else core), col)

    def yx_peer(d):
        y_, x_ = lax.rem(y + d[0], Y_DIM), lax.rem(col + d[1], X_DIM)
        return y_ * X_DIM + x_, (device(z, y_, core), x_)

    n_zc, n_yx = 2 * Z_DIM - 1, Y_DIM * X_DIM - 1
    me_q = z * 2 + core
    me_s = y * X_DIM + col

    def load_p():
        return pltpu.make_async_copy(p_hbm, pg.at[col], load_sem.at[4])

    def load_t(b, k):
        rows = pl.ds(pl.multiple_of(b * ROWS_OWN, ROWS_OWN), ROWS_OWN)
        return pltpu.make_async_copy(t_hbm.at[rows, :], t_ref.at[rows, :], load_sem.at[k])

    load_p().start()
    order = (col, left, right, across)
    for k, b in enumerate(order):
        load_t(b, k).start()

    barrier = pltpu.get_barrier_semaphore()

    def greet(peer):
        pl.semaphore_signal(barrier, inc=1, device_id=peer, device_id_type=MESH)

    def each(lo, hi, f):
        def step(d, c):
            f(d)
            return c

        lax.fori_loop(lo, hi, step, 0)

    z_next, z_prev = (lax.rem(z + d, Z_DIM) for d in (1, Z_DIM - 1))
    y_next, y_prev = (lax.rem(y + d, Y_DIM) for d in (1, Y_DIM - 1))
    near = (
        (row, right), (row, left), (device(z, y_next, core), col), (device(z, y_prev, core), col),
        (device(z_next, y, core), col), (device(z_prev, y, core), col),
    )
    for peer in near:
        greet(peer)
    greet(sibling)

    load_p().wait()
    pl.semaphore_wait(barrier, 7)

    def introduce(peer, k=0):
        pl.semaphore_signal(know_sem.at[k], inc=1, device_id=peer, device_id_type=MESH)

    def remote(src, dst, send, recv, peer):
        return pltpu.make_async_remote_copy(
            src_ref=src, dst_ref=dst, send_sem=send, recv_sem=recv, device_id=peer, device_id_type=MESH
        )

    top, bottom = pl.ds(0, HALF), pl.ds(HALF, HALF)

    def ring(k, block, part, to):
        src = pg.at[block, part, :]
        return remote(src, pg.at[block, part, :], gsend.at[k], grecv.at[k], (row, to))

    ring(0, col, top, right).start()
    ring(1, col, bottom, left).start()
    ring(2, col, bottom, right).start()
    ring(3, col, top, left).start()

    for peer in near:
        introduce(peer)

    own = pg[col]
    gram = inner(own, own, HIGHEST)
    gbuf[...] = gram.reshape(NB // 8, 8, NB)

    pl.semaphore_wait(know_sem.at[0], len(near))
    introduce((device(lax.rem(z + 2, Z_DIM), y, core), col), 1)
    introduce((device(lax.rem(z + Z_DIM - 2, Z_DIM), y, core), col), 1)
    for to in (right, left, across):
        introduce((row, to), 1)

    def split_t(k, b):
        load_t(b, k).wait()
        rows = pl.ds(pl.multiple_of(b * ROWS_OWN, ROWS_OWN), ROWS_OWN)
        hi, lo = split(t_ref[rows, :])
        thl[0, rows, :] = hi
        thl[1, rows, :] = lo

    def rows_of(b):
        return pl.ds(pl.multiple_of(b * ROWS_OWN, ROWS_OWN), ROWS_OWN)

    def split_p(b):
        hi, lo = split(pg[b])
        phl_ref[rows_of(b), 0:NB] = hi
        phl_ref[rows_of(b), NB : 2 * NB] = lo

    def product(b, h, first=False):
        at = pl.ds(pl.multiple_of(h * (COLS_OWN // 2), COLS_OWN // 2), COLS_OWN // 2)
        hi, lo = phl_ref[rows_of(b), 0:NB], phl_ref[rows_of(b), NB : 2 * NB]
        th = thl[0, rows_of(b), at]
        s = inner(hi, th) + inner(lo, th) + inner(hi, thl[1, rows_of(b), at])
        for j in range(2):
            t = s[:, NB * j : NB * (j + 1)].reshape(16, 8, NB)
            tiles = pl.ds(pl.multiple_of(h * CHIPS + 16 * j, 16), 16)
            sbuf[tiles] = t if first else sbuf[tiles] + t

    split_t(0, order[0])
    split_p(col)
    product(col, 0, True)
    product(col, 1, True)

    ring(0, left, top, right).wait_recv()
    ring(4, left, top, right).start()
    ring(1, right, bottom, left).wait_recv()
    ring(5, right, bottom, left).start()

    pl.semaphore_wait(know_sem.at[1], 2 + X_DIM - 1)
    each(1, Y_DIM, lambda d: introduce((device(z, lax.rem(y + d, Y_DIM), core), col), 2))
    introduce(sibling, 2)

    for k, d in enumerate(far_first(Y_DIM, X_DIM)):
        t, peer = yx_peer(d)
        remote(gbuf.at[t], abuf.at[k], esend.at[0], erecv.at[0], peer).start()

    def received(k, buf):
        remote(buf, buf, esend.at[k], erecv.at[k], sibling).wait_recv()

    def sent(k, buf):
        remote(buf, buf, esend.at[k], erecv.at[k], sibling).wait_send()

    split_t(1, order[1])
    split_t(2, order[2])
    split_t(3, order[3])

    received(0, abuf)
    bbuf[me_q] = gbuf[me_s] + jnp.sum(abuf[...], axis=0)

    pl.semaphore_wait(know_sem.at[2], Y_DIM)

    for d in far_first(Z_DIM, 2):
        remote(bbuf.at[me_q], bbuf.at[me_q], esend.at[1], erecv.at[1], zc_peer(d)).start()

    ring(2, left, bottom, right).wait_recv()
    split_p(left)
    product(left, 0)
    product(left, 1)
    ring(3, right, top, left).wait_recv()
    split_p(right)
    product(right, 0)
    product(right, 1)

    ring(4, across, top, right).wait_recv()
    ring(5, across, bottom, left).wait_recv()
    split_p(across)
    product(across, 1 - core)

    mine = pl.ds(pl.multiple_of(core * CHIPS, CHIPS), CHIPS)
    other = pl.ds(pl.multiple_of((1 - core) * CHIPS, CHIPS), CHIPS)
    swap = remote(sbuf.at[other], cbuf, esend.at[3], erecv.at[3], sibling)
    swap.start()
    product(across, core)
    swap.wait_recv()
    sred[...] = sbuf[mine] + cbuf[...]

    for k, d in enumerate(far_first(Z_DIM, Y_DIM)):
        m, peer = chip_peer(d)
        remote(sred.at[m], rbuf.at[k], esend.at[4], erecv.at[4], peer).start()

    received(1, bbuf.at[pl.ds(0, n_zc)])
    gfull[me_s] = jnp.sum(bbuf[...], axis=0)

    for d in far_first(Y_DIM, X_DIM):
        remote(gfull.at[me_s], gfull.at[me_s], esend.at[2], erecv.at[2], yx_peer(d)[1]).start()

    received(4, rbuf)
    slot = core * CHIPS + chip
    sfull[slot] = sred[chip] + jnp.sum(rbuf[...], axis=0)

    for d in far_first(Z_DIM, Y_DIM):
        remote(sfull.at[slot], sfull.at[slot], esend.at[5], erecv.at[5], chip_peer(d)[1]).start()
    received(2, gfull.at[pl.ds(0, n_yx)])
    factor_gram([gfull[i] for i in range(NB // 8)], r_ref, y_ref)

    for k, block, part, to in (
        (0, col, top, right), (1, col, bottom, left), (2, col, bottom, right),
        (3, col, top, left), (4, left, top, right), (5, right, bottom, left),
    ):
        ring(k, block, part, to).wait_send()
    sent(0, abuf)
    sent(1, bbuf.at[pl.ds(0, n_zc)])
    sent(2, gfull.at[pl.ds(0, n_yx)])
    swap.wait_send()
    sent(4, rbuf)

    inv_t = y_ref[...]
    both = jnp.concatenate([inv_t, inner(inv_t, inv_t, HIGHEST)], axis=0)

    def finish(h):
        tiles = [sfull[pl.ds(pl.multiple_of(h * CHIPS + 16 * j, 16), 16)].reshape(NB, NB) for j in range(2)]
        wx = jnp.dot(both, jnp.concatenate(tiles, axis=1), precision=HIGHEST, preferred_element_type=F32)
        at = pl.ds(pl.multiple_of(h * (COLS_OWN // 2), COLS_OWN // 2), COLS_OWN // 2)
        w_ref[:, at] = wx[:NB]
        hi, lo = split(wx[NB:])
        xh_ref[0:NB, at] = hi
        xh_ref[NB : 2 * NB, at] = hi
        xl_ref[:, at] = lo

    received(5, sfull.at[pl.ds(0, CHIPS - 1)])
    last = remote(sfull.at[mine], sfull.at[mine], esend.at[6], erecv.at[6], sibling)
    last.start()
    finish(core)
    sent(5, sfull.at[pl.ds(0, CHIPS - 1)])
    last.wait()
    finish(1 - core)


def rest_kernel(norm_scale, r_ref, w_ref, xh_ref, xl_ref, phl_ref, t_ref, rs_hbm, ws_hbm, out_hbm, rs, ws, obuf, sem, tiles=8):
    size = ROWS_OWN * X_DIM // tiles

    def put(i):
        return pltpu.make_async_copy(obuf.at[i], out_hbm.at[pl.ds(i * size, size), :], sem.at[i])

    scaled = [pltpu.make_async_copy(rs, rs_hbm, sem.at[tiles]), pltpu.make_async_copy(ws, ws_hbm, sem.at[tiles + 1])]
    rs[...] = r_ref[...] * norm_scale
    ws[...] = w_ref[...] * norm_scale
    for copy in scaled:
        copy.start()
    for i in range(tiles):
        rows = slice(i * size, (i + 1) * size)
        q = jnp.dot(phl_ref[rows, :], xh_ref[...], preferred_element_type=F32)
        q = q + jnp.dot(phl_ref[rows, 0:NB], xl_ref[...], preferred_element_type=F32)
        obuf[i] = t_ref[rows, :] - q
        put(i).start()
    for copy in scaled:
        copy.wait()
    for i in range(tiles):
        put(i).wait()


def body(panel_block, trailing):
    total_rows = panel_block.shape[0] * lax.axis_size("row") * lax.axis_size("col")
    norm_scale = 1.0 / math.sqrt(total_rows)
    rows = trailing.shape[0]
    vm = pl.BlockSpec(memory_space=pltpu.VMEM)
    anym = pl.BlockSpec(memory_space=pl.ANY)

    def out(shape, dtype):
        return jax.ShapeDtypeStruct(shape, dtype)

    parts = pl.pallas_call(
        main_kernel,
        out_shape=[
            out((NB, NB), F32), out((NB, COLS_OWN), F32), out((2 * NB, COLS_OWN), BF16), out((NB, COLS_OWN), BF16),
            out((rows, 2 * NB), BF16), out((rows, COLS_OWN), F32),
        ],
        in_specs=[pl.BlockSpec(memory_space=pltpu.HBM)] * 2,
        out_specs=[vm] * 6,
        scratch_shapes=[
            pltpu.VMEM((X_DIM, ROWS_OWN, NB), F32),
            pltpu.VMEM((2, rows, COLS_OWN), BF16),
            pltpu.VMEM((16, 8, NB), F32),
            pltpu.VMEM((15, 8, NB), F32),
            pltpu.VMEM((16, 8, NB), F32),
            pltpu.VMEM((16, 8, NB), F32),
            pltpu.VMEM((NB, NB), F32),
            pltpu.VMEM((64, 8, NB), F32),
            pltpu.VMEM((32, 8, NB), F32),
            pltpu.VMEM((32, 8, NB), F32),
            pltpu.VMEM((31, 8, NB), F32),
            pltpu.VMEM((64, 8, NB), F32),
            pltpu.SemaphoreType.DMA((5,)),
            pltpu.SemaphoreType.DMA((6,)),
            pltpu.SemaphoreType.DMA((6,)),
            pltpu.SemaphoreType.DMA((7,)),
            pltpu.SemaphoreType.DMA((7,)),
            pltpu.SemaphoreType.REGULAR((3,)),
        ],
        compiler_params=pltpu.CompilerParams(collective_id=0, has_side_effects=True, vmem_limit_bytes=40 << 20),
    )(*(pltpu.with_memory_space_constraint(a, pltpu.HBM) for a in (panel_block, trailing)))
    return pl.pallas_call(
        lambda *refs: rest_kernel(norm_scale, *refs),
        out_shape=[out((NB, NB), F32), out((NB, COLS_OWN), F32), out((rows, COLS_OWN), F32)],
        in_specs=[vm] * 6,
        out_specs=[anym] * 3,
        scratch_shapes=[
            pltpu.VMEM((NB, NB), F32), pltpu.VMEM((NB, COLS_OWN), F32),
            pltpu.VMEM((8, rows // 8, COLS_OWN), F32), pltpu.SemaphoreType.DMA((10,)),
        ],
        compiler_params=pltpu.CompilerParams(vmem_limit_bytes=40 << 20),
    )(*parts)


def solution(mesh):
    in_specs = (P(("row", "col"), None), P("row", "col"))
    out_specs = (P(), P(None, "col"), P("row", "col"))
    return jax.shard_map(body, mesh=mesh, in_specs=in_specs, out_specs=out_specs, check_vma=False)
```

```python
import math

import jax
import jax.numpy as jnp
from jax import lax
from jax.experimental import pallas as pl
from jax.experimental.pallas import tpu as pltpu
from jax.sharding import PartitionSpec as P

F32 = jnp.float32
BF16 = jnp.bfloat16
MESH = pl.DeviceIdType.MESH
HIGHEST = lax.Precision.HIGHEST
NB = 128
Y_DIM, Z_DIM, X_DIM = 4, 8, 4
CHIPS = Y_DIM * Z_DIM
ROWS_OWN = 512
COLS_OWN = 512
HALF = ROWS_OWN // 2


def lane_spread(v, c):
    return jnp.broadcast_to(v[:, c : c + 1], (8, NB))


def row_spread(v, j):
    return jnp.broadcast_to(v[j : j + 1, :], (8, NB))


def factor_gram(g, r_ref, y_ref):
    sub = lax.broadcasted_iota(jnp.int32, (8, NB), 0)
    lane = lax.broadcasted_iota(jnp.int32, (8, NB), 1)
    n = NB // 8
    left = [g[i] for i in range(n)]
    right = [jnp.where(lane == sub + 8 * i, 1.0, 0.0) for i in range(n)]
    for k in range(n):
        v, w = left[k], right[k]
        diag = [lane_spread(v, 8 * k + j) for j in range(8)]
        more = k + 1 < n
        if more:
            v2, w2 = left[k + 1], right[k + 1]
            diag2 = [lane_spread(v2, 8 * k + j) for j in range(8)]
        pivots = jnp.ones((8, NB), F32)
        p = row_spread(diag[0], 0)
        for j in range(8):
            r0 = pltpu.reciprocal(p, approx=True)
            e = 2.0 - p * r0
            r = r0 * e
            pivots = jnp.where(sub == j, p, pivots)
            rows = [row_spread(diag[jj], j) for jj in range(j + 1, 8)]
            if rows:
                p = row_spread(diag[j + 1], j + 1) - (rows[0] * rows[0] * r0) * e
            m = jnp.where(sub > j, diag[j], 0.0) * r
            vj, wj = row_spread(v, j), row_spread(w, j)
            v, w = v - m * vj, w - m * wj
            if more:
                m2 = diag2[j] * r
                v2, w2 = v2 - m2 * vj, w2 - m2 * wj
            for jj, row in zip(range(j + 1, 8), rows):
                diag[jj] = diag[jj] - m * row
                if more:
                    diag2[jj] = diag2[jj] - m2 * row
        scale = lax.rsqrt(pivots)
        u = jnp.where(lane >= 8 * k + sub, v * scale, 0.0)
        z = w * scale
        r_ref[8 * k : 8 * k + 8, :] = u
        y_ref[8 * k : 8 * k + 8, :] = z
        if more:
            left[k + 1], right[k + 1] = v2, w2
        if k + 2 < n:
            uz = jnp.concatenate([u, z], axis=1)
            high = uz.astype(BF16).astype(F32)
            mid = (uz - high).astype(BF16).astype(F32)
            low = uz - high - mid
            one = [high, high, mid, high, mid, low]
            two = [high, mid, high, low, mid, high]
            drop = inner(
                jnp.concatenate([q[:, :NB] for q in one], axis=0).astype(BF16),
                jnp.concatenate(two, axis=0).astype(BF16),
            )
            for i in range(k + 2, n):
                left[i] = left[i] - drop[8 * i : 8 * i + 8, :NB]
                right[i] = right[i] - drop[8 * i : 8 * i + 8, NB:]


def split(x):
    hi = x.astype(BF16)
    return hi, (x - hi.astype(F32)).astype(BF16)


def inner(a, b, precision=None):
    return lax.dot_general(a, b, (((0,), (0,)), ((), ())), precision=precision, preferred_element_type=F32)


def main_kernel(
    p_hbm, t_hbm,
    r_ref, w_ref, xh_ref, xl_ref, phl_ref, t_ref,
    pg, thl, gbuf, abuf, bbuf, gfull, y_ref, sbuf, cbuf, sred, rbuf, sfull,
    load_sem, gsend, grecv, esend, erecv, know_sem,
):
    row = lax.axis_index("row")
    col = lax.axis_index("col")
    core = lax.rem(row, 2)
    chip = lax.div(row, 2)
    y = lax.rem(chip, Y_DIM)
    z = lax.div(chip, Y_DIM)
    right, left, across = (lax.rem(col + d, X_DIM) for d in (1, 3, 2))

    def device(z_, y_, core_):
        return (z_ * Y_DIM + y_) * 2 + core_

    sibling = (row + 1 - 2 * core, col)

    def hops(n, d):
        return min(d, n - d)

    def far_first(n, m):
        pairs = [(i, j) for i in range(n) for j in range(m) if i or j]
        return sorted(pairs, key=lambda p: -hops(n, p[0]) - hops(m, p[1]))

    def chip_peer(d):
        z_, y_ = lax.rem(z + d[0], Z_DIM), lax.rem(y + d[1], Y_DIM)
        return z_ * Y_DIM + y_, (device(z_, y_, core), col)

    def zc_peer(d):
        z_ = lax.rem(z + d[0], Z_DIM)
        return (device(z_, y, 1 - core if d[1] else core), col)

    def yx_peer(d):
        y_, x_ = lax.rem(y + d[0], Y_DIM), lax.rem(col + d[1], X_DIM)
        return y_ * X_DIM + x_, (device(z, y_, core), x_)

    n_zc, n_yx = 2 * Z_DIM - 1, Y_DIM * X_DIM - 1
    me_q = z * 2 + core
    me_s = y * X_DIM + col

    def load_p():
        return pltpu.make_async_copy(p_hbm, pg.at[col], load_sem.at[4])

    def load_t(b, k):
        rows = pl.ds(pl.multiple_of(b * ROWS_OWN, ROWS_OWN), ROWS_OWN)
        return pltpu.make_async_copy(t_hbm.at[rows, :], t_ref.at[rows, :], load_sem.at[k])

    load_p().start()
    order = (col, left, right, across)
    for k, b in enumerate(order):
        load_t(b, k).start()

    barrier = pltpu.get_barrier_semaphore()

    def greet(peer):
        pl.semaphore_signal(barrier, inc=1, device_id=peer, device_id_type=MESH)

    def each(lo, hi, f):
        def step(d, c):
            f(d)
            return c

        lax.fori_loop(lo, hi, step, 0)

    z_next, z_prev = (lax.rem(z + d, Z_DIM) for d in (1, Z_DIM - 1))
    y_next, y_prev = (lax.rem(y + d, Y_DIM) for d in (1, Y_DIM - 1))
    near = (
        (row, right), (row, left), (device(z, y_next, core), col), (device(z, y_prev, core), col),
        (device(z_next, y, core), col), (device(z_prev, y, core), col),
    )
    for peer in near:
        greet(peer)
    greet(sibling)

    load_p().wait()
    pl.semaphore_wait(barrier, 7)

    def introduce(peer, k=0):
        pl.semaphore_signal(know_sem.at[k], inc=1, device_id=peer, device_id_type=MESH)

    def remote(src, dst, send, recv, peer):
        return pltpu.make_async_remote_copy(
            src_ref=src, dst_ref=dst, send_sem=send, recv_sem=recv, device_id=peer, device_id_type=MESH
        )

    top, bottom = pl.ds(0, HALF), pl.ds(HALF, HALF)

    def ring(k, block, part, to):
        src = pg.at[block, part, :]
        return remote(src, pg.at[block, part, :], gsend.at[k], grecv.at[k], (row, to))

    ring(0, col, top, right).start()
    ring(1, col, bottom, left).start()
    ring(2, col, bottom, right).start()
    ring(3, col, top, left).start()

    for peer in near:
        introduce(peer)

    own = pg[col]
    gram = inner(own, own, HIGHEST)
    gbuf[...] = gram.reshape(NB // 8, 8, NB)

    pl.semaphore_wait(know_sem.at[0], len(near))
    introduce((device(lax.rem(z + 2, Z_DIM), y, core), col), 1)
    introduce((device(lax.rem(z + Z_DIM - 2, Z_DIM), y, core), col), 1)
    for to in (right, left, across):
        introduce((row, to), 1)

    def split_t(k, b):
        load_t(b, k).wait()
        rows = pl.ds(pl.multiple_of(b * ROWS_OWN, ROWS_OWN), ROWS_OWN)
        hi, lo = split(t_ref[rows, :])
        thl[0, rows, :] = hi
        thl[1, rows, :] = lo

    def rows_of(b):
        return pl.ds(pl.multiple_of(b * ROWS_OWN, ROWS_OWN), ROWS_OWN)

    def split_p(b):
        hi, lo = split(pg[b])
        phl_ref[rows_of(b), 0:NB] = hi
        phl_ref[rows_of(b), NB : 2 * NB] = lo

    def product(b, h, first=False):
        at = pl.ds(pl.multiple_of(h * (COLS_OWN // 2), COLS_OWN // 2), COLS_OWN // 2)
        hi, lo = phl_ref[rows_of(b), 0:NB], phl_ref[rows_of(b), NB : 2 * NB]
        th = thl[0, rows_of(b), at]
        s = inner(hi, th) + inner(lo, th) + inner(hi, thl[1, rows_of(b), at])
        for j in range(2):
            t = s[:, NB * j : NB * (j + 1)].reshape(16, 8, NB)
            tiles = pl.ds(pl.multiple_of(h * CHIPS + 16 * j, 16), 16)
            sbuf[tiles] = t if first else sbuf[tiles] + t

    split_t(0, order[0])
    split_p(col)
    product(col, 0, True)
    product(col, 1, True)
    pl.semaphore_wait(know_sem.at[1], 2 + X_DIM - 1)
    each(1, Y_DIM, lambda d: introduce((device(z, lax.rem(y + d, Y_DIM), core), col), 2))
    introduce(sibling, 2)

    for k, d in enumerate(far_first(Y_DIM, X_DIM)):
        t, peer = yx_peer(d)
        remote(gbuf.at[t], abuf.at[k], esend.at[0], erecv.at[0], peer).start()

    def received(k, buf):
        remote(buf, buf, esend.at[k], erecv.at[k], sibling).wait_recv()

    def sent(k, buf):
        remote(buf, buf, esend.at[k], erecv.at[k], sibling).wait_send()

    ring(0, left, top, right).wait_recv()
    ring(4, left, top, right).start()
    ring(1, right, bottom, left).wait_recv()
    ring(5, right, bottom, left).start()

    split_t(1, order[1])
    split_t(2, order[2])
    split_t(3, order[3])

    ring(2, left, bottom, right).wait_recv()
    split_p(left)
    product(left, 0)
    product(left, 1)
    ring(3, right, top, left).wait_recv()
    split_p(right)
    product(right, 0)
    product(right, 1)

    received(0, abuf)
    bbuf[me_q] = gbuf[me_s] + jnp.sum(abuf[...], axis=0)

    pl.semaphore_wait(know_sem.at[2], Y_DIM)

    for d in far_first(Z_DIM, 2):
        remote(bbuf.at[me_q], bbuf.at[me_q], esend.at[1], erecv.at[1], zc_peer(d)).start()

    ring(4, across, top, right).wait_recv()
    ring(5, across, bottom, left).wait_recv()
    split_p(across)
    product(across, 1 - core)

    mine = pl.ds(pl.multiple_of(core * CHIPS, CHIPS), CHIPS)
    other = pl.ds(pl.multiple_of((1 - core) * CHIPS, CHIPS), CHIPS)
    swap = remote(sbuf.at[other], cbuf, esend.at[3], erecv.at[3], sibling)
    swap.start()
    product(across, core)
    swap.wait_recv()
    sred[...] = sbuf[mine] + cbuf[...]

    for k, d in enumerate(far_first(Z_DIM, Y_DIM)):
        m, peer = chip_peer(d)
        remote(sred.at[m], rbuf.at[k], esend.at[4], erecv.at[4], peer).start()

    received(1, bbuf.at[pl.ds(0, n_zc)])
    gfull[me_s] = jnp.sum(bbuf[...], axis=0)

    for d in far_first(Y_DIM, X_DIM):
        remote(gfull.at[me_s], gfull.at[me_s], esend.at[2], erecv.at[2], yx_peer(d)[1]).start()

    received(4, rbuf)
    slot = core * CHIPS + chip
    sfull[slot] = sred[chip] + jnp.sum(rbuf[...], axis=0)

    for d in far_first(Z_DIM, Y_DIM):
        remote(sfull.at[slot], sfull.at[slot], esend.at[5], erecv.at[5], chip_peer(d)[1]).start()
    received(2, gfull.at[pl.ds(0, n_yx)])
    factor_gram([gfull[i] for i in range(NB // 8)], r_ref, y_ref)

    for k, block, part, to in (
        (0, col, top, right), (1, col, bottom, left), (2, col, bottom, right),
        (3, col, top, left), (4, left, top, right), (5, right, bottom, left),
    ):
        ring(k, block, part, to).wait_send()
    sent(0, abuf)
    sent(1, bbuf.at[pl.ds(0, n_zc)])
    sent(2, gfull.at[pl.ds(0, n_yx)])
    swap.wait_send()
    sent(4, rbuf)

    inv_t = y_ref[...]
    both = jnp.concatenate([inv_t, inner(inv_t, inv_t, HIGHEST)], axis=0)

    def finish(h):
        tiles = [sfull[pl.ds(pl.multiple_of(h * CHIPS + 16 * j, 16), 16)].reshape(NB, NB) for j in range(2)]
        wx = jnp.dot(both, jnp.concatenate(tiles, axis=1), precision=HIGHEST, preferred_element_type=F32)
        at = pl.ds(pl.multiple_of(h * (COLS_OWN // 2), COLS_OWN // 2), COLS_OWN // 2)
        w_ref[:, at] = wx[:NB]
        hi, lo = split(wx[NB:])
        xh_ref[0:NB, at] = hi
        xh_ref[NB : 2 * NB, at] = hi
        xl_ref[:, at] = lo

    received(5, sfull.at[pl.ds(0, CHIPS - 1)])
    last = remote(sfull.at[mine], sfull.at[mine], esend.at[6], erecv.at[6], sibling)
    last.start()
    finish(core)
    sent(5, sfull.at[pl.ds(0, CHIPS - 1)])
    last.wait()
    finish(1 - core)


def rest_kernel(norm_scale, r_ref, w_ref, xh_ref, xl_ref, phl_ref, t_ref, rs_hbm, ws_hbm, out_hbm, rs, ws, obuf, sem, tiles=8):
    size = ROWS_OWN * X_DIM // tiles

    def put(i):
        return pltpu.make_async_copy(obuf.at[i], out_hbm.at[pl.ds(i * size, size), :], sem.at[i])

    scaled = [pltpu.make_async_copy(rs, rs_hbm, sem.at[tiles]), pltpu.make_async_copy(ws, ws_hbm, sem.at[tiles + 1])]
    rs[...] = r_ref[...] * norm_scale
    ws[...] = w_ref[...] * norm_scale
    for copy in scaled:
        copy.start()
    for i in range(tiles):
        rows = slice(i * size, (i + 1) * size)
        q = jnp.dot(phl_ref[rows, :], xh_ref[...], preferred_element_type=F32)
        q = q + jnp.dot(phl_ref[rows, 0:NB], xl_ref[...], preferred_element_type=F32)
        obuf[i] = t_ref[rows, :] - q
        put(i).start()
    for copy in scaled:
        copy.wait()
    for i in range(tiles):
        put(i).wait()


def body(panel_block, trailing):
    total_rows = panel_block.shape[0] * lax.axis_size("row") * lax.axis_size("col")
    norm_scale = 1.0 / math.sqrt(total_rows)
    rows = trailing.shape[0]
    vm = pl.BlockSpec(memory_space=pltpu.VMEM)
    anym = pl.BlockSpec(memory_space=pl.ANY)

    def out(shape, dtype):
        return jax.ShapeDtypeStruct(shape, dtype)

    parts = pl.pallas_call(
        main_kernel,
        out_shape=[
            out((NB, NB), F32), out((NB, COLS_OWN), F32), out((2 * NB, COLS_OWN), BF16), out((NB, COLS_OWN), BF16),
            out((rows, 2 * NB), BF16), out((rows, COLS_OWN), F32),
        ],
        in_specs=[pl.BlockSpec(memory_space=pltpu.HBM)] * 2,
        out_specs=[vm] * 6,
        scratch_shapes=[
            pltpu.VMEM((X_DIM, ROWS_OWN, NB), F32),
            pltpu.VMEM((2, rows, COLS_OWN), BF16),
            pltpu.VMEM((16, 8, NB), F32),
            pltpu.VMEM((15, 8, NB), F32),
            pltpu.VMEM((16, 8, NB), F32),
            pltpu.VMEM((16, 8, NB), F32),
            pltpu.VMEM((NB, NB), F32),
            pltpu.VMEM((64, 8, NB), F32),
            pltpu.VMEM((32, 8, NB), F32),
            pltpu.VMEM((32, 8, NB), F32),
            pltpu.VMEM((31, 8, NB), F32),
            pltpu.VMEM((64, 8, NB), F32),
            pltpu.SemaphoreType.DMA((5,)),
            pltpu.SemaphoreType.DMA((6,)),
            pltpu.SemaphoreType.DMA((6,)),
            pltpu.SemaphoreType.DMA((7,)),
            pltpu.SemaphoreType.DMA((7,)),
            pltpu.SemaphoreType.REGULAR((3,)),
        ],
        compiler_params=pltpu.CompilerParams(collective_id=0, has_side_effects=True, vmem_limit_bytes=40 << 20),
    )(*(pltpu.with_memory_space_constraint(a, pltpu.HBM) for a in (panel_block, trailing)))
    return pl.pallas_call(
        lambda *refs: rest_kernel(norm_scale, *refs),
        out_shape=[out((NB, NB), F32), out((NB, COLS_OWN), F32), out((rows, COLS_OWN), F32)],
        in_specs=[vm] * 6,
        out_specs=[anym] * 3,
        scratch_shapes=[
            pltpu.VMEM((NB, NB), F32), pltpu.VMEM((NB, COLS_OWN), F32),
            pltpu.VMEM((8, rows // 8, COLS_OWN), F32), pltpu.SemaphoreType.DMA((10,)),
        ],
        compiler_params=pltpu.CompilerParams(vmem_limit_bytes=40 << 20),
    )(*parts)


def solution(mesh):
    in_specs = (P(("row", "col"), None), P("row", "col"))
    out_specs = (P(), P(None, "col"), P("row", "col"))
    return jax.shard_map(body, mesh=mesh, in_specs=in_specs, out_specs=out_specs, check_vma=False)
```

```python
import math

import jax
import jax.numpy as jnp
from jax import lax
from jax.experimental import pallas as pl
from jax.experimental.pallas import tpu as pltpu
from jax.sharding import PartitionSpec as P

F32 = jnp.float32
BF16 = jnp.bfloat16
MESH = pl.DeviceIdType.MESH
HIGHEST = lax.Precision.HIGHEST
NB = 128
Y_DIM, Z_DIM, X_DIM = 4, 8, 4
CHIPS = Y_DIM * Z_DIM
ROWS_OWN = 512
COLS_OWN = 512
HALF = ROWS_OWN // 2


def lane_spread(v, c):
    return jnp.broadcast_to(v[:, c : c + 1], (8, NB))


def row_spread(v, j):
    return jnp.broadcast_to(v[j : j + 1, :], (8, NB))


def factor_gram(g, r_ref, y_ref):
    sub = lax.broadcasted_iota(jnp.int32, (8, NB), 0)
    lane = lax.broadcasted_iota(jnp.int32, (8, NB), 1)
    n = NB // 8
    left = [g[i] for i in range(n)]
    right = [jnp.where(lane == sub + 8 * i, 1.0, 0.0) for i in range(n)]
    for k in range(n):
        v, w = left[k], right[k]
        diag = [lane_spread(v, 8 * k + j) for j in range(8)]
        more = k + 1 < n
        if more:
            v2, w2 = left[k + 1], right[k + 1]
            diag2 = [lane_spread(v2, 8 * k + j) for j in range(8)]
        pivots = jnp.ones((8, NB), F32)
        p = row_spread(diag[0], 0)
        for j in range(8):
            r0 = pltpu.reciprocal(p, approx=True)
            e = 2.0 - p * r0
            r = r0 * e
            pivots = jnp.where(sub == j, p, pivots)
            rows = [row_spread(diag[jj], j) for jj in range(j + 1, 8)]
            if rows:
                p = row_spread(diag[j + 1], j + 1) - (rows[0] * rows[0] * r0) * e
            m = jnp.where(sub > j, diag[j], 0.0) * r
            vj, wj = row_spread(v, j), row_spread(w, j)
            v, w = v - m * vj, w - m * wj
            if more:
                m2 = diag2[j] * r
                v2, w2 = v2 - m2 * vj, w2 - m2 * wj
            for jj, row in zip(range(j + 1, 8), rows):
                diag[jj] = diag[jj] - m * row
                if more:
                    diag2[jj] = diag2[jj] - m2 * row
        scale = lax.rsqrt(pivots)
        u = jnp.where(lane >= 8 * k + sub, v * scale, 0.0)
        z = w * scale
        r_ref[8 * k : 8 * k + 8, :] = u
        y_ref[8 * k : 8 * k + 8, :] = z
        if more:
            left[k + 1], right[k + 1] = v2, w2
        if k + 2 < n:
            uz = jnp.concatenate([u, z], axis=1)
            high = uz.astype(BF16).astype(F32)
            mid = (uz - high).astype(BF16).astype(F32)
            low = uz - high - mid
            one = [high, high, mid, high, mid, low]
            two = [high, mid, high, low, mid, high]
            drop = inner(
                jnp.concatenate([q[:, :NB] for q in one], axis=0).astype(BF16),
                jnp.concatenate(two, axis=0).astype(BF16),
            )
            for i in range(k + 2, n):
                left[i] = left[i] - drop[8 * i : 8 * i + 8, :NB]
                right[i] = right[i] - drop[8 * i : 8 * i + 8, NB:]


def split(x):
    hi = x.astype(BF16)
    return hi, (x - hi.astype(F32)).astype(BF16)


def inner(a, b, precision=None):
    return lax.dot_general(a, b, (((0,), (0,)), ((), ())), precision=precision, preferred_element_type=F32)


def main_kernel(
    p_hbm, t_hbm,
    r_ref, w_ref, xh_ref, xl_ref, phl_ref, t_ref,
    pg, thl, gbuf, abuf, bbuf, gfull, y_ref, sbuf, cbuf, sred, rbuf, sfull,
    load_sem, gsend, grecv, esend, erecv, know_sem,
):
    row = lax.axis_index("row")
    col = lax.axis_index("col")
    core = lax.rem(row, 2)
    chip = lax.div(row, 2)
    y = lax.rem(chip, Y_DIM)
    z = lax.div(chip, Y_DIM)
    right, left, across = (lax.rem(col + d, X_DIM) for d in (1, 3, 2))

    def device(z_, y_, core_):
        return (z_ * Y_DIM + y_) * 2 + core_

    sibling = (row + 1 - 2 * core, col)

    def hops(n, d):
        return min(d, n - d)

    def far_first(n, m):
        pairs = [(i, j) for i in range(n) for j in range(m) if i or j]
        return sorted(pairs, key=lambda p: -hops(n, p[0]) - hops(m, p[1]))

    def chip_peer(d):
        z_, y_ = lax.rem(z + d[0], Z_DIM), lax.rem(y + d[1], Y_DIM)
        return z_ * Y_DIM + y_, (device(z_, y_, core), col)

    def zc_peer(d):
        z_ = lax.rem(z + d[0], Z_DIM)
        return (device(z_, y, 1 - core if d[1] else core), col)

    def yx_peer(d):
        y_, x_ = lax.rem(y + d[0], Y_DIM), lax.rem(col + d[1], X_DIM)
        return y_ * X_DIM + x_, (device(z, y_, core), x_)

    n_zc, n_yx = 2 * Z_DIM - 1, Y_DIM * X_DIM - 1
    me_q = z * 2 + core
    me_s = y * X_DIM + col

    def load_p():
        return pltpu.make_async_copy(p_hbm, pg.at[col], load_sem.at[4])

    def load_t(b, k):
        rows = pl.ds(pl.multiple_of(b * ROWS_OWN, ROWS_OWN), ROWS_OWN)
        return pltpu.make_async_copy(t_hbm.at[rows, :], t_ref.at[rows, :], load_sem.at[k])

    load_p().start()
    barrier = pltpu.get_barrier_semaphore()

    def greet(peer):
        pl.semaphore_signal(barrier, inc=1, device_id=peer, device_id_type=MESH)

    def each(lo, hi, f):
        def step(d, c):
            f(d)
            return c

        lax.fori_loop(lo, hi, step, 0)

    z_next, z_prev = (lax.rem(z + d, Z_DIM) for d in (1, Z_DIM - 1))
    y_next, y_prev = (lax.rem(y + d, Y_DIM) for d in (1, Y_DIM - 1))
    near = (
        (row, right), (row, left), (device(z, y_next, core), col), (device(z, y_prev, core), col),
        (device(z_next, y, core), col), (device(z_prev, y, core), col),
    )
    for peer in near:
        greet(peer)
    greet(sibling)

    order = (col, left, right, across)
    for k, b in enumerate(order):
        load_t(b, k).start()

    load_p().wait()
    pl.semaphore_wait(barrier, 7)

    def introduce(peer, k=0):
        pl.semaphore_signal(know_sem.at[k], inc=1, device_id=peer, device_id_type=MESH)

    def remote(src, dst, send, recv, peer):
        return pltpu.make_async_remote_copy(
            src_ref=src, dst_ref=dst, send_sem=send, recv_sem=recv, device_id=peer, device_id_type=MESH
        )

    top, bottom = pl.ds(0, HALF), pl.ds(HALF, HALF)

    def ring(k, block, part, to):
        src = pg.at[block, part, :]
        return remote(src, pg.at[block, part, :], gsend.at[k], grecv.at[k], (row, to))

    ring(0, col, top, right).start()
    ring(1, col, bottom, left).start()
    ring(2, col, bottom, right).start()
    ring(3, col, top, left).start()

    for peer in near:
        introduce(peer)

    own = pg[col]
    gram = inner(own, own, HIGHEST)
    gbuf[...] = gram.reshape(NB // 8, 8, NB)

    pl.semaphore_wait(know_sem.at[0], len(near))
    introduce((device(lax.rem(z + 2, Z_DIM), y, core), col), 1)
    introduce((device(lax.rem(z + Z_DIM - 2, Z_DIM), y, core), col), 1)
    for to in (right, left, across):
        introduce((row, to), 1)

    def split_t(k, b):
        load_t(b, k).wait()
        rows = pl.ds(pl.multiple_of(b * ROWS_OWN, ROWS_OWN), ROWS_OWN)
        hi, lo = split(t_ref[rows, :])
        thl[0, rows, :] = hi
        thl[1, rows, :] = lo

    def rows_of(b):
        return pl.ds(pl.multiple_of(b * ROWS_OWN, ROWS_OWN), ROWS_OWN)

    def split_p(b):
        hi, lo = split(pg[b])
        phl_ref[rows_of(b), 0:NB] = hi
        phl_ref[rows_of(b), NB : 2 * NB] = lo

    def product(b, h, first=False):
        at = pl.ds(pl.multiple_of(h * (COLS_OWN // 2), COLS_OWN // 2), COLS_OWN // 2)
        hi, lo = phl_ref[rows_of(b), 0:NB], phl_ref[rows_of(b), NB : 2 * NB]
        th = thl[0, rows_of(b), at]
        s = inner(hi, th) + inner(lo, th) + inner(hi, thl[1, rows_of(b), at])
        for j in range(2):
            t = s[:, NB * j : NB * (j + 1)].reshape(16, 8, NB)
            tiles = pl.ds(pl.multiple_of(h * CHIPS + 16 * j, 16), 16)
            sbuf[tiles] = t if first else sbuf[tiles] + t

    split_t(0, order[0])
    split_p(col)
    product(col, 0, True)
    product(col, 1, True)
    pl.semaphore_wait(know_sem.at[1], 2 + X_DIM - 1)
    each(1, Y_DIM, lambda d: introduce((device(z, lax.rem(y + d, Y_DIM), core), col), 2))
    introduce(sibling, 2)

    for k, d in enumerate(far_first(Y_DIM, X_DIM)):
        t, peer = yx_peer(d)
        remote(gbuf.at[t], abuf.at[k], esend.at[0], erecv.at[0], peer).start()

    def received(k, buf):
        remote(buf, buf, esend.at[k], erecv.at[k], sibling).wait_recv()

    def sent(k, buf):
        remote(buf, buf, esend.at[k], erecv.at[k], sibling).wait_send()

    ring(0, left, top, right).wait_recv()
    ring(4, left, top, right).start()
    ring(1, right, bottom, left).wait_recv()
    ring(5, right, bottom, left).start()

    split_t(1, order[1])
    split_t(2, order[2])
    split_t(3, order[3])

    ring(2, left, bottom, right).wait_recv()
    split_p(left)
    product(left, 0)
    product(left, 1)
    ring(3, right, top, left).wait_recv()
    split_p(right)
    product(right, 0)
    product(right, 1)

    received(0, abuf)
    bbuf[me_q] = gbuf[me_s] + jnp.sum(abuf[...], axis=0)

    pl.semaphore_wait(know_sem.at[2], Y_DIM)

    for d in far_first(Z_DIM, 2):
        remote(bbuf.at[me_q], bbuf.at[me_q], esend.at[1], erecv.at[1], zc_peer(d)).start()

    ring(4, across, top, right).wait_recv()
    ring(5, across, bottom, left).wait_recv()
    split_p(across)
    product(across, 1 - core)

    mine = pl.ds(pl.multiple_of(core * CHIPS, CHIPS), CHIPS)
    other = pl.ds(pl.multiple_of((1 - core) * CHIPS, CHIPS), CHIPS)
    swap = remote(sbuf.at[other], cbuf, esend.at[3], erecv.at[3], sibling)
    swap.start()
    product(across, core)
    swap.wait_recv()
    sred[...] = sbuf[mine] + cbuf[...]

    for k, d in enumerate(far_first(Z_DIM, Y_DIM)):
        m, peer = chip_peer(d)
        remote(sred.at[m], rbuf.at[k], esend.at[4], erecv.at[4], peer).start()

    received(1, bbuf.at[pl.ds(0, n_zc)])
    gfull[me_s] = jnp.sum(bbuf[...], axis=0)

    for d in far_first(Y_DIM, X_DIM):
        remote(gfull.at[me_s], gfull.at[me_s], esend.at[2], erecv.at[2], yx_peer(d)[1]).start()

    received(4, rbuf)
    slot = core * CHIPS + chip
    sfull[slot] = sred[chip] + jnp.sum(rbuf[...], axis=0)

    for d in far_first(Z_DIM, Y_DIM):
        remote(sfull.at[slot], sfull.at[slot], esend.at[5], erecv.at[5], chip_peer(d)[1]).start()
    received(2, gfull.at[pl.ds(0, n_yx)])
    factor_gram([gfull[i] for i in range(NB // 8)], r_ref, y_ref)

    for k, block, part, to in (
        (0, col, top, right), (1, col, bottom, left), (2, col, bottom, right),
        (3, col, top, left), (4, left, top, right), (5, right, bottom, left),
    ):
        ring(k, block, part, to).wait_send()
    sent(0, abuf)
    sent(1, bbuf.at[pl.ds(0, n_zc)])
    sent(2, gfull.at[pl.ds(0, n_yx)])
    swap.wait_send()
    sent(4, rbuf)

    inv_t = y_ref[...]
    both = jnp.concatenate([inv_t, inner(inv_t, inv_t, HIGHEST)], axis=0)

    def finish(h):
        tiles = [sfull[pl.ds(pl.multiple_of(h * CHIPS + 16 * j, 16), 16)].reshape(NB, NB) for j in range(2)]
        wx = jnp.dot(both, jnp.concatenate(tiles, axis=1), precision=HIGHEST, preferred_element_type=F32)
        at = pl.ds(pl.multiple_of(h * (COLS_OWN // 2), COLS_OWN // 2), COLS_OWN // 2)
        w_ref[:, at] = wx[:NB]
        hi, lo = split(wx[NB:])
        xh_ref[0:NB, at] = hi
        xh_ref[NB : 2 * NB, at] = hi
        xl_ref[:, at] = lo

    received(5, sfull.at[pl.ds(0, CHIPS - 1)])
    last = remote(sfull.at[mine], sfull.at[mine], esend.at[6], erecv.at[6], sibling)
    last.start()
    finish(core)
    sent(5, sfull.at[pl.ds(0, CHIPS - 1)])
    last.wait()
    finish(1 - core)


def rest_kernel(norm_scale, r_ref, w_ref, xh_ref, xl_ref, phl_ref, t_ref, rs_hbm, ws_hbm, out_hbm, rs, ws, obuf, sem, tiles=8):
    size = ROWS_OWN * X_DIM // tiles

    def put(i):
        return pltpu.make_async_copy(obuf.at[i], out_hbm.at[pl.ds(i * size, size), :], sem.at[i])

    scaled = [pltpu.make_async_copy(rs, rs_hbm, sem.at[tiles]), pltpu.make_async_copy(ws, ws_hbm, sem.at[tiles + 1])]
    rs[...] = r_ref[...] * norm_scale
    ws[...] = w_ref[...] * norm_scale
    for copy in scaled:
        copy.start()
    for i in range(tiles):
        rows = slice(i * size, (i + 1) * size)
        q = jnp.dot(phl_ref[rows, :], xh_ref[...], preferred_element_type=F32)
        q = q + jnp.dot(phl_ref[rows, 0:NB], xl_ref[...], preferred_element_type=F32)
        obuf[i] = t_ref[rows, :] - q
        put(i).start()
    for copy in scaled:
        copy.wait()
    for i in range(tiles):
        put(i).wait()


def body(panel_block, trailing):
    total_rows = panel_block.shape[0] * lax.axis_size("row") * lax.axis_size("col")
    norm_scale = 1.0 / math.sqrt(total_rows)
    rows = trailing.shape[0]
    vm = pl.BlockSpec(memory_space=pltpu.VMEM)
    anym = pl.BlockSpec(memory_space=pl.ANY)

    def out(shape, dtype):
        return jax.ShapeDtypeStruct(shape, dtype)

    parts = pl.pallas_call(
        main_kernel,
        out_shape=[
            out((NB, NB), F32), out((NB, COLS_OWN), F32), out((2 * NB, COLS_OWN), BF16), out((NB, COLS_OWN), BF16),
            out((rows, 2 * NB), BF16), out((rows, COLS_OWN), F32),
        ],
        in_specs=[pl.BlockSpec(memory_space=pltpu.HBM)] * 2,
        out_specs=[vm] * 6,
        scratch_shapes=[
            pltpu.VMEM((X_DIM, ROWS_OWN, NB), F32),
            pltpu.VMEM((2, rows, COLS_OWN), BF16),
            pltpu.VMEM((16, 8, NB), F32),
            pltpu.VMEM((15, 8, NB), F32),
            pltpu.VMEM((16, 8, NB), F32),
            pltpu.VMEM((16, 8, NB), F32),
            pltpu.VMEM((NB, NB), F32),
            pltpu.VMEM((64, 8, NB), F32),
            pltpu.VMEM((32, 8, NB), F32),
            pltpu.VMEM((32, 8, NB), F32),
            pltpu.VMEM((31, 8, NB), F32),
            pltpu.VMEM((64, 8, NB), F32),
            pltpu.SemaphoreType.DMA((5,)),
            pltpu.SemaphoreType.DMA((6,)),
            pltpu.SemaphoreType.DMA((6,)),
            pltpu.SemaphoreType.DMA((7,)),
            pltpu.SemaphoreType.DMA((7,)),
            pltpu.SemaphoreType.REGULAR((3,)),
        ],
        compiler_params=pltpu.CompilerParams(collective_id=0, has_side_effects=True, vmem_limit_bytes=40 << 20),
    )(*(pltpu.with_memory_space_constraint(a, pltpu.HBM) for a in (panel_block, trailing)))
    return pl.pallas_call(
        lambda *refs: rest_kernel(norm_scale, *refs),
        out_shape=[out((NB, NB), F32), out((NB, COLS_OWN), F32), out((rows, COLS_OWN), F32)],
        in_specs=[vm] * 6,
        out_specs=[anym] * 3,
        scratch_shapes=[
            pltpu.VMEM((NB, NB), F32), pltpu.VMEM((NB, COLS_OWN), F32),
            pltpu.VMEM((8, rows // 8, COLS_OWN), F32), pltpu.SemaphoreType.DMA((10,)),
        ],
        compiler_params=pltpu.CompilerParams(vmem_limit_bytes=40 << 20),
    )(*parts)


def solution(mesh):
    in_specs = (P(("row", "col"), None), P("row", "col"))
    out_specs = (P(), P(None, "col"), P("row", "col"))
    return jax.shard_map(body, mesh=mesh, in_specs=in_specs, out_specs=out_specs, check_vma=False)
```
